256 devices in a mesh: hst: 4 (over x), local: 64 (over z, y, core).
Axes of the slice: x: 4, y: 4, z: 8, core: 2. Of those that a mesh axis runs over, the one named last changes fastest.
Arguments:
- table_rows: float32 [4, 8192, 128], P('hst', 'local'), may hold values from -2.5 to 2.5
- row_accum: float32 [4, 8192], P('hst', 'local'), may hold values from 0.1 to 1
- row_ids: int32 [4, 8, 32768], P('hst'), may hold values from 0 to 8191
- sketch_bits: int32 [4, 8, 32768], P('hst'), may hold values from 0 to 1
- cross_u: bfloat16 [512, 512], replicated, may hold values from -0.25 to 0.25
- cross_v: bfloat16 [512, 512], replicated, may hold values from -0.25 to 0.25
- cross_bias: float32 [512], replicated, may hold values from -3 to 3
- cotangent: bfloat16 [32768, 512], P(('hst', 'local')), may hold values from -6 to 6
Outputs:
- crossed: bfloat16 [32768, 512], P(('hst', 'local'))
- new_rows: float32 [4, 8192, 128], P('hst', 'local')
- new_accum: float32 [4, 8192], P('hst', 'local')
The draws below stay inside these ranges and needn't reach their ends.
All inputs are finite; a program needn't handle non-finite values.
Results may differ from the reference program's by a relative error of at most 0.0023.
The reference program's roundings to bfloat16 on the way (of `low`, `mixed` and `back_low`) count: a program that leaves them out, or rounds other values in their place, can miss the bound.
Values sent between devices are 32-bit elements; how exact they have to be, the bound alone decides.
No kernel may reach another device: no remote copies, remote signals or barrier semaphores. Data moves between devices by JAX's collectives and lax.ppermute only.
A program may use at most 128 MiB of HBM per device.

```python
import math
import jax
import jax.numpy as jnp
import numpy as np
from jax import lax

E = 128
R = 512
BAG = 8
TABLES = 4
ROWS = 8192
BATCH = 32768
D = 512


def set_ends(values, key, least, high):
    longest = values.shape.index(max(values.shape))
    spots = []
    for shift in (0, 1):
        where = [jax.random.randint(jax.random.fold_in(key, axis), (), 0, length) for axis, length in enumerate(values.shape)]
        where[longest] = (where[longest] + shift) % values.shape[longest]
        spots.append(tuple(where))
    return values.at[spots[0]].set(least).at[spots[1]].set(high)


def block_levels(stream_key, shape, split, low, top_value):
    loudness = 1.0
    for position, blocks in split:
        heights = jax.random.uniform(jax.random.fold_in(jax.random.fold_in(stream_key, 6), position), (blocks,), jnp.float32, low / len(split), top_value / len(split))
        loudness = loudness * jnp.repeat(jnp.exp(heights), shape[position] // blocks).reshape((-1,) + (1,) * (len(shape) - 1 - position))
    return loudness


def rank_bounds(amount, skew):
    loads = [(1 << 20) // math.isqrt(rank ** skew) + 1 for rank in range(1, amount + 1)]
    deviation = 1 + sum(loads) // (1 << 30)
    return np.cumsum(np.array([max(1, weight // deviation) for weight in loads]))


def skewed_ids(rng, shape, count, skew):
    listing = rank_bounds(count, skew)
    ticket = jax.random.randint(jax.random.fold_in(rng, 1), shape, 0, int(listing[count - 1]))
    standing = jnp.searchsorted(jnp.asarray(listing, jnp.int32), ticket, side="right")
    return jax.random.permutation(jax.random.fold_in(rng, 2), count)[standing].astype(jnp.int32)


def centred(own_key, extent, spread, most, split=(), dtype=jnp.bfloat16):
    drawn = jax.random.normal(own_key, extent, jnp.float32) * spread
    if len(split) > 0:
        drawn = block_levels(own_key, extent, split, -0.22, 0.18) * drawn
    return jnp.clip(drawn, min=-most, max=most).astype(dtype)


def setup_inputs(seed: int = 0) -> dict:
    keys = jax.random.split(jax.random.key(seed), 9)
    table_rows = centred(keys[0], (TABLES, ROWS, E), 0.35, 2.5, ((0, 4), (1, 64)), jnp.float32)
    row_accum = jnp.clip(jnp.exp(math.log(1.0) - 2.3025851 * jax.random.uniform(keys[1], (TABLES, ROWS), jnp.float32) ** block_levels(keys[1], (TABLES, ROWS), ((0, 4), (1, 64)), -0.2, 0.2)), 0.1, 1.0)
    row_ids = set_ends(skewed_ids(keys[2], (TABLES, BAG, BATCH), ROWS, 2), jax.random.fold_in(keys[2], 3), 0, ROWS - 1).astype(jnp.int32)
    sketch_bits = set_ends(jax.random.randint(keys[3], (TABLES, BAG, BATCH), 0, 2), jax.random.fold_in(keys[3], 1), 0, 1).astype(jnp.int32)
    cross_u = centred(keys[4], (D, R), D ** -0.5, 0.25)
    cross_v = centred(keys[5], (R, D), R ** -0.5, 0.25)
    cross_bias = centred(keys[6], (D,), 0.5, 3.0, (), jnp.float32)
    cotangent = centred(keys[7], (BATCH, D), 1.0, 6.0, ((0, 256),))
    return dict(table_rows=table_rows, row_accum=row_accum, row_ids=row_ids, sketch_bits=sketch_bits, cross_u=cross_u, cross_v=cross_v, cross_bias=cross_bias, cotangent=cotangent)


learn_rate = 0.1

def pool_table(operands):
    table, id_block, sign_block = operands
    picked = table[id_block]
    return lax.optimization_barrier(jnp.sum(picked * sign_block[:, :, None], axis=0))

def grad_table(operands):
    grads, id_block, sign_block = operands
    terms = sign_block[:, :, None] * grads[None, :, :]
    return jax.ops.segment_sum(terms.reshape(-1, E), id_block.reshape(-1), num_segments=ROWS)

def reference(table_rows, row_accum, row_ids, sketch_bits, cross_u, cross_v, cross_bias, cotangent):
    signs = (2 * sketch_bits - 1).astype(jnp.float32)
    pooled = lax.map(pool_table, (table_rows, row_ids, signs))
    base_x = pooled.transpose(1, 0, 2).reshape(BATCH, TABLES * E)
    low = jnp.dot(base_x.astype(jnp.bfloat16), cross_u, preferred_element_type=jnp.float32).astype(jnp.bfloat16)
    scale = jnp.dot(low, cross_v, preferred_element_type=jnp.float32) + cross_bias
    crossed = (base_x * scale + base_x).astype(jnp.bfloat16)
    upstream = cotangent.astype(jnp.float32)
    mixed = (upstream * base_x).astype(jnp.bfloat16)
    back_low = jnp.dot(mixed, cross_v.T, preferred_element_type=jnp.float32).astype(jnp.bfloat16)
    grad_x = upstream * (scale + 1.0) + jnp.dot(back_low, cross_u.T, preferred_element_type=jnp.float32)
    grad_tables = grad_x.reshape(BATCH, TABLES, E).transpose(1, 0, 2)
    row_grads = lax.map(grad_table, (grad_tables, row_ids, signs))
    new_accum = row_accum + lax.optimization_barrier(jnp.mean(row_grads * row_grads, axis=2))
    new_rows = table_rows - learn_rate * row_grads / jnp.sqrt(new_accum)[:, :, None]
    return (crossed, new_rows, new_accum)
```

```python
import functools

import jax
import jax.numpy as jnp
from jax import lax
from jax.experimental import pallas as pl
from jax.experimental.pallas import tpu as pltpu
from jax.sharding import Mesh, PartitionSpec as P

learn_rate = 0.1
NX, NZ, NY, NC = 4, 8, 4, 2
RB, SB, E, BAG = 128, 128, 128, 8
SIZES = {"hst": NX, "z": NZ, "y": NY, "core": NC}
HALF_ROWS = NZ * RB
SAMPLES_Y = NX * SB
F32, BF16 = jnp.float32, jnp.bfloat16
VMEM = pltpu.CompilerParams(vmem_limit_bytes=40 << 20)


def move(array, axis, step):
    n = SIZES[axis]
    return lax.ppermute(array, axis, [(i, (i + step) % n) for i in range(n)])


def call(kernel, out_shapes, *operands, flops=0, moved=0):
    shapes = [jax.ShapeDtypeStruct(s, d) for s, d in out_shapes]
    return pl.pallas_call(
        kernel,
        out_shape=shapes,
        compiler_params=VMEM,
        cost_estimate=pl.CostEstimate(flops=flops, bytes_accessed=moved or 1 << 20, transcendentals=0),
    )(*operands)


def split_terms(value):
    high = value.astype(BF16)
    return jnp.concatenate([high, (value - high.astype(F32)).astype(BF16)], axis=1)


def counts_kernel(pos, ids_ref, bits_ref, out_ref):
    z, y, c = pos[1], pos[2], pos[3]
    rows16 = lax.broadcasted_iota(jnp.int32, (16, SB), 0).astype(jnp.int16)
    for dx in range(NX):
        x = (pos[0] + dx) & (NX - 1)
        ids = ids_ref[x, 0, 0, 0]
        rel = (((ids >> 7) & 1) ^ c) * HALF_ROWS + (((ids >> 10) - z) & (NZ - 1)) * RB + (ids & (RB - 1))
        rel = jnp.where(((ids >> 8) & (NY - 1)) == y, rel, -1)
        sign = (2 * bits_ref[x, 0, 0, 0] - 1).astype(F32)
        rels = [jnp.broadcast_to(rel[k : k + 1], (16, SB)).astype(jnp.int16) for k in range(BAG)]
        signs = [jnp.broadcast_to(sign[k : k + 1], (16, SB)).astype(BF16) for k in range(BAG)]

        def step(r, carry):
            here = rows16 + (r * 16).astype(jnp.int16)
            total = jnp.where(rels[0] == here, signs[0], BF16(0))
            for k in range(1, BAG):
                total = total + jnp.where(rels[k] == here, signs[k], BF16(0))
            out_ref[pl.ds(pl.multiple_of(r * 16, 16), 16), dx * SB : (dx + 1) * SB] = total
            return carry

        lax.fori_loop(0, NC * HALF_ROWS // 16, step, 0, unroll=16)


def counts_of(pos, ids, bits, dy):
    spec = pl.BlockSpec(
        (NX, 1, 1, 1, BAG, SB), lambda i, p: (0, p[1], (p[2] + dy) & (NY - 1), p[3], 0, 0)
    )
    return pl.pallas_call(
        counts_kernel,
        grid_spec=pltpu.PrefetchScalarGridSpec(
            num_scalar_prefetch=1,
            grid=(1,),
            in_specs=[spec, spec],
            out_specs=pl.BlockSpec((NC * HALF_ROWS, SAMPLES_Y), lambda i, p: (0, 0)),
        ),
        out_shape=jax.ShapeDtypeStruct((NC * HALF_ROWS, SAMPLES_Y), BF16),
        compiler_params=VMEM,
        cost_estimate=pl.CostEstimate(
            flops=3 * BAG * NC * HALF_ROWS * SAMPLES_Y, bytes_accessed=4 << 20, transcendentals=0
        ),
    )(pos, ids, bits)


def forward_kernel(own, p1, m1, p2, m2, up, down):
    up[:RB] = p1[...]
    up[RB:] = p2[: RB // 2]
    down[:RB] = m1[...]
    down[RB:] = m2[RB // 2 :]


def gather_kernel(own, p1, m1, p2, m2, p3, m3, out):
    h = RB // 2
    out[0:RB] = own[...]
    out[RB : 2 * RB] = m1[...]
    out[2 * RB : 3 * RB] = m2[...]
    out[3 * RB : 4 * RB] = m3[:RB]
    out[4 * RB : 4 * RB + h] = p3[RB:]
    out[4 * RB + h : 5 * RB] = m3[RB:]
    out[5 * RB : 6 * RB] = p3[:RB]
    out[6 * RB : 7 * RB] = p2[...]
    out[7 * RB : 8 * RB] = p1[...]


def pool_kernel(with_base, rows, c0, c1, c2, c3, *refs):
    base, outs, (totals,) = (refs[:4], refs[4:8], refs[8:]) if with_base else (None, refs[:4], refs[4:])
    step = pl.program_id(0)
    terms = split_terms(rows[...])
    for d, c in enumerate((c0, c1, c2, c3)):
        part = lax.dot_general(terms, c[...], (((0,), (0,)), ((), ())), preferred_element_type=F32)
        part = part[:E] + part[E:]

        @pl.when(step == 0)
        def _():
            totals[d] = part

        @pl.when(step == pl.num_programs(0) - 1)
        def _():
            for i in range(NX):
                s = slice(i * SB, (i + 1) * SB)
                value = (totals[d, :, s] + part[:, s]).T
                if with_base:
                    value = value + base[d][s]
                outs[d][s] = value


def pool(rows, counts, half, base=()):
    kb = HALF_ROWS // 2
    whole = pl.BlockSpec((SAMPLES_Y, E), lambda i: (0, 0))
    return pl.pallas_call(
        functools.partial(pool_kernel, len(base) > 0),
        grid=(2,),
        in_specs=[pl.BlockSpec((kb, E), lambda i: (i, 0))]
        + [pl.BlockSpec((kb, SAMPLES_Y), lambda i: (2 * half + i, 0))] * NY
        + [whole] * len(base),
        out_specs=[whole] * NY,
        out_shape=[jax.ShapeDtypeStruct((SAMPLES_Y, E), F32)] * NY,
        scratch_shapes=[pltpu.VMEM((NY, E, SAMPLES_Y), F32)],
        compiler_params=VMEM,
        cost_estimate=pl.CostEstimate(
            flops=4 * HALF_ROWS * NY * SAMPLES_Y * E, bytes_accessed=6 << 20, transcendentals=0
        ),
    )(rows, *counts, *base)


def owners_kernel(a, b, c, d, o0, o1, o2, o3):
    for i, out in enumerate((o0, o1, o2, o3)):
        s = slice(i * SB, (i + 1) * SB)
        out[...] = (a[s] + b[s]) + (c[s] + d[s])


def cross_kernel(pos, b0, b1, b2, b3, u, v, bias, cot, crossed, g0, g1, g2, g3, x_ref):
    def columns(d):
        return pl.ds(pl.multiple_of(((pos[0] - d) & (NX - 1)) * E, E), E)

    for d, b in enumerate((b0, b1, b2, b3)):
        x_ref[:, columns(d)] = b[...]
    base_x = x_ref[...]
    low = jnp.dot(base_x.astype(BF16), u[...], preferred_element_type=F32).astype(BF16)
    scale = jnp.dot(low, v[...], preferred_element_type=F32) + bias[...]
    crossed[...] = (base_x * scale + base_x).astype(BF16)
    upstream = cot[...].astype(F32)
    mixed = (upstream * base_x).astype(BF16)
    last = (((1,), (1,)), ((), ()))
    back_low = lax.dot_general(mixed, v[...], last, preferred_element_type=F32).astype(BF16)
    x_ref[...] = upstream * (scale + 1.0) + lax.dot_general(
        back_low, u[...], last, preferred_element_type=F32
    )
    for d, g in enumerate((g0, g1, g2, g3)):
        g[...] = x_ref[:, columns(d)]


def cross(pos, parts, u, v, bias, cot):
    vm = pl.BlockSpec(memory_space=pltpu.VMEM)
    return pl.pallas_call(
        cross_kernel,
        in_specs=[pl.BlockSpec(memory_space=pltpu.SMEM)] + [vm] * 8,
        out_specs=[vm] * 5,
        out_shape=[jax.ShapeDtypeStruct(cot.shape, BF16)] + [jax.ShapeDtypeStruct((SB, E), F32)] * NX,
        scratch_shapes=[pltpu.VMEM(cot.shape, F32)],
        compiler_params=VMEM,
        cost_estimate=pl.CostEstimate(flops=8 * SB * 512 * 512, bytes_accessed=2 << 20, transcendentals=0),
    )(pos, *parts, u, v, bias, cot)


def stack_kernel(a, b, c, d, out):
    for i, ref in enumerate((a, b, c, d)):
        out[i * SB : (i + 1) * SB] = ref[...]


def grads_kernel(c0, c1, c2, c3, g0, g1, g2, g3, out, terms):
    @pl.when(pl.program_id(0) == 0)
    def _():
        for d, g in enumerate((g0, g1, g2, g3)):
            terms[d] = split_terms(g[...])

    total = None
    for d, c in enumerate((c0, c1, c2, c3)):
        part = jnp.dot(c[...], terms[d], preferred_element_type=F32)
        total = part if total is None else total + part
    out[...] = total[:, :E] + total[:, E:]


def grads(counts, parts, half):
    rows = 256
    steps = HALF_ROWS // rows
    return pl.pallas_call(
        grads_kernel,
        grid=(steps,),
        in_specs=[pl.BlockSpec((rows, SAMPLES_Y), lambda i: (steps * half + i, 0))] * NY
        + [pl.BlockSpec((SAMPLES_Y, E), lambda i: (0, 0))] * NY,
        out_specs=pl.BlockSpec((rows, E), lambda i: (i, 0)),
        out_shape=jax.ShapeDtypeStruct((HALF_ROWS, E), F32),
        scratch_shapes=[pltpu.VMEM((NY, SAMPLES_Y, 2 * E), BF16)],
        compiler_params=VMEM,
        cost_estimate=pl.CostEstimate(
            flops=4 * HALF_ROWS * NY * SAMPLES_Y * E, bytes_accessed=6 << 20, transcendentals=0
        ),
    )(*counts, *parts)


def far_kernel(a, b, up, down, keep):
    h = RB // 2
    up[...] = a[3 * RB : 4 * RB + h] + b[3 * RB : 4 * RB + h]
    down[:RB] = a[5 * RB : 6 * RB] + b[5 * RB : 6 * RB]
    down[RB:] = a[4 * RB + h : 5 * RB] + b[4 * RB + h : 5 * RB]
    keep[: 3 * RB] = a[: 3 * RB] + b[: 3 * RB]
    keep[3 * RB :] = a[6 * RB :] + b[6 * RB :]


def near_kernel(keep, up, down, p1, p2, m2, m1):
    h = RB // 2
    p1[...] = keep[RB : 2 * RB] + up[:RB]
    p2[:h] = keep[2 * RB : 2 * RB + h] + up[RB:]
    p2[h:] = keep[2 * RB + h : 3 * RB]
    m2[:h] = keep[3 * RB : 3 * RB + h]
    m2[h:] = keep[3 * RB + h : 4 * RB] + down[RB:]
    m1[...] = keep[4 * RB :] + down[:RB]


def update_kernel(keep, a, b, c, d, rows, accum, new_rows, new_accum):
    grad = keep[:RB] + ((a[...] + b[...]) + (c[...] + d[...]))
    mean = jnp.sum(grad * grad, axis=1, keepdims=True) * (1.0 / E)
    mean_row = jnp.broadcast_to(mean, (RB, E)).T[:1]
    total = accum[...] + mean_row
    new_accum[...] = total
    total_column = jnp.broadcast_to(total, (E, RB)).T
    new_rows[...] = rows[...] - learn_rate * grad / jnp.sqrt(total_column)


def per_device(
    table_rows, row_accum, row_ids, sketch_bits, cross_u, cross_v, cross_bias, cotangent
):
    pos = jnp.stack([lax.axis_index(a) for a in ("hst", "z", "y", "core")]).astype(jnp.int32)
    own = table_rows[0]

    def by_owner(entries):
        return entries[0].reshape(BAG, -1, SB).transpose(1, 0, 2).reshape(NX, NZ, NY, NC, BAG, SB)

    ids, bits = by_owner(row_ids), by_owner(sketch_bits)
    p1, m1 = move(own, "z", 1), move(own, "z", -1)
    p2, m2 = move(own, "z", 2), move(own, "z", -2)
    counts = [counts_of(pos, ids, bits, d) for d in range(NY)]
    third = (RB + RB // 2, E)
    up, down = call(forward_kernel, [(third, F32)] * 2, own, p1, m1, p2, m2)
    p3, m3 = move(up, "z", 2), move(down, "z", -2)
    (rows,) = call(gather_kernel, [((HALF_ROWS, E), F32)], own, p1, m1, p2, m2, p3, m3)
    other_rows = move(rows, "core", 1)
    pooled = pool(rows, counts, 0)
    pooled = pool(other_rows, counts, 1, pooled)
    block = ((SB, E), F32)
    mine = call(
        owners_kernel,
        [block] * NX,
        pooled[0],
        move(pooled[1], "y", 1),
        move(pooled[2], "y", 2),
        move(pooled[3], "y", -1),
    )
    parts = [mine[0]] + [move(mine[d], "hst", d) for d in range(1, NX)]
    crossed, *grad_parts = cross(
        pos, parts, cross_u, cross_v, cross_bias.reshape(1, -1), cotangent
    )
    back = [grad_parts[0]] + [move(grad_parts[d], "hst", -d) for d in range(1, NX)]
    (bag_grads,) = call(stack_kernel, [((SAMPLES_Y, E), F32)], *back)
    all_grads = [bag_grads] + [move(bag_grads, "y", -d) for d in range(1, NY)]
    other_half = grads(counts, all_grads, 1)
    from_other = move(other_half, "core", 1)
    own_half = grads(counts, all_grads, 0)
    up, down, keep = call(
        far_kernel, [(third, F32)] * 2 + [((5 * RB, E), F32)], own_half, from_other
    )
    near = call(near_kernel, [block] * 4, keep, move(up, "z", 2), move(down, "z", -2))
    sums = [move(a, "z", s) for a, s in zip(near, (1, 2, -2, -1))]
    new_rows, new_accum = call(
        update_kernel, [block, ((1, RB), F32)], keep, *sums, own, row_accum
    )
    return (crossed, new_rows[None], new_accum)


def solution(mesh):
    grid = Mesh(mesh.devices.reshape(NX, NZ, NY, NC), ("hst", "z", "y", "core"))
    local = ("z", "y", "core")
    in_specs = (
        P("hst", local, None),
        P("hst", local),
        P("hst", None, None),
        P("hst", None, None),
        P(),
        P(),
        P(),
        P(("hst",) + local, None),
    )
    out_specs = (P(("hst",) + local, None), P("hst", local, None), P("hst", local))
    return jax.shard_map(
        per_device, mesh=grid, in_specs=in_specs, out_specs=out_specs, check_vma=False
    )
```

```python
import functools

import jax
import jax.numpy as jnp
from jax import lax
from jax.experimental import pallas as pl
from jax.experimental.pallas import tpu as pltpu
from jax.sharding import Mesh, PartitionSpec as P

learn_rate = 0.1
NX, NZ, NY, NC = 4, 8, 4, 2
RB, SB, E, BAG = 128, 128, 128, 8
SIZES = {"hst": NX, "z": NZ, "y": NY, "core": NC}
HALF_ROWS = NZ * RB
NEAR = 5 * RB
RADIX = 17
SAMPLES_Y = NX * SB
F32, BF16 = jnp.float32, jnp.bfloat16
VMEM = pltpu.CompilerParams(vmem_limit_bytes=40 << 20)


def move(array, axis, step):
    n = SIZES[axis]
    return lax.ppermute(array, axis, [(i, (i + step) % n) for i in range(n)])


def call(kernel, out_shapes, *operands, flops=0, moved=0):
    shapes = [jax.ShapeDtypeStruct(s, d) for s, d in out_shapes]
    return pl.pallas_call(
        kernel,
        out_shape=shapes,
        compiler_params=VMEM,
        cost_estimate=pl.CostEstimate(flops=flops, bytes_accessed=moved or 1 << 20, transcendentals=0),
    )(*operands)


def split_terms(value):
    high = value.astype(BF16)
    return jnp.concatenate([high, (value - high.astype(F32)).astype(BF16)], axis=1)


def entries_kernel(pos, ids_hbm, bits_hbm, spot_ref, value_ref, ids, bits, sems):
    z, y, c = pos[1], pos[2], pos[3]
    copies = [
        pltpu.make_async_copy(source.at[:, z, :, c], target, sems.at[i])
        for i, (source, target) in enumerate(((ids_hbm, ids), (bits_hbm, bits)))
    ]
    for copy in copies:
        copy.start()
    for copy in copies:
        copy.wait()
    for dy in range(NY):
        for dx in range(NX):
            at = (pos[0] + dx) & (NX - 1), (y + dy) & (NY - 1)
            row = ids[at]
            spot = (((row >> 10) - z + 2) & (NZ - 1)) * RB + (row & (RB - 1))
            spot_ref[dy, dx] = jnp.where(((row >> 8) & (NY - 1)) == y, spot, -1)
            other = (((row >> 7) & 1) ^ c).astype(F32)
            value_ref[dy, dx] = (2 * bits[at] - 1).astype(F32) * (1.0 + (RADIX - 1) * other)


def entries_of(pos, ids, bits):
    shape = (NX, NY, BAG, SB)
    return pl.pallas_call(
        entries_kernel,
        in_specs=[pl.BlockSpec(memory_space=pltpu.SMEM)] + [pl.BlockSpec(memory_space=pltpu.HBM)] * 2,
        out_specs=[pl.BlockSpec(memory_space=pltpu.VMEM)] * 2,
        out_shape=[jax.ShapeDtypeStruct(shape, jnp.int32), jax.ShapeDtypeStruct(shape, F32)],
        scratch_shapes=[pltpu.VMEM(shape, jnp.int32)] * 2 + [pltpu.SemaphoreType.DMA((2,))],
        compiler_params=VMEM,
        cost_estimate=pl.CostEstimate(flops=1 << 20, bytes_accessed=1 << 19, transcendentals=0),
    )(pos, ids, bits)


def counts_kernel(spot_ref, value_ref, out_ref):
    rows16 = lax.broadcasted_iota(jnp.int32, (16, SB), 0).astype(jnp.int16)
    for dx in range(NX):
        spots = [jnp.broadcast_to(spot_ref[dx, k : k + 1], (16, SB)).astype(jnp.int16) for k in range(BAG)]
        values = [jnp.broadcast_to(value_ref[dx, k : k + 1], (16, SB)).astype(BF16) for k in range(BAG)]
        columns = slice(dx * SB, (dx + 1) * SB)

        def step(r, carry):
            here = rows16 + (r * 16).astype(jnp.int16)
            terms = [jnp.where(s == here, v, BF16(0)) for s, v in zip(spots, values)]
            while len(terms) > 1:
                terms = [a + b for a, b in zip(terms[::2], terms[1::2])]
            high = (terms[0] * BF16(1.0 / RADIX) + BF16(192)) - BF16(192)
            at = pl.multiple_of(r * 16, 16)
            out_ref[pl.ds(at, 16), columns] = terms[0] - high * BF16(RADIX)
            out_ref[pl.ds(HALF_ROWS + at, 16), columns] = high
            return carry

        lax.fori_loop(0, HALF_ROWS // 16, step, 0, unroll=16)


def counts_of(entries, dy, *after):
    vm = pl.BlockSpec(memory_space=pltpu.VMEM)
    spec = pl.BlockSpec((None, NX, BAG, SB), lambda i: (dy, 0, 0, 0))
    return pl.pallas_call(
        lambda s, v, *rest: counts_kernel(s, v, rest[-1]),
        grid=(1,),
        in_specs=[spec, spec] + [pl.BlockSpec(memory_space=pl.ANY)] * len(after),
        out_specs=pl.BlockSpec(memory_space=pltpu.VMEM),
        out_shape=jax.ShapeDtypeStruct((NC * HALF_ROWS, SAMPLES_Y), BF16),
        compiler_params=VMEM,
        cost_estimate=pl.CostEstimate(flops=1 << 28, bytes_accessed=2 << 20, transcendentals=0),
    )(*entries, *after)


def forward_kernel(own, p1, m1, p2, m2, *refs):
    near, up, down = refs[-3:]
    for i, ref in enumerate((p2, p1, own, m1, m2)):
        near[i * RB : (i + 1) * RB] = ref[...]
    up[:RB] = p1[...]
    up[RB:] = p2[: RB // 2]
    down[:RB] = m1[...]
    down[RB:] = m2[RB // 2 :]


def far_rows_kernel(p3, m3, *refs):
    far = refs[-1]
    h = RB // 2
    far[:RB] = m3[:RB]
    far[RB : RB + h] = p3[RB:]
    far[RB + h : 2 * RB] = m3[RB:]
    far[2 * RB :] = p3[:RB]


def call_after(kernel, out_shapes, operands, after):
    vm, anywhere = pl.BlockSpec(memory_space=pltpu.VMEM), pl.BlockSpec(memory_space=pl.ANY)
    return pl.pallas_call(
        kernel,
        in_specs=[vm] * len(operands) + [anywhere] * len(after),
        out_specs=[vm] * len(out_shapes),
        out_shape=[jax.ShapeDtypeStruct(s, F32) for s in out_shapes],
        compiler_params=VMEM,
        cost_estimate=pl.CostEstimate(flops=0, bytes_accessed=1 << 18, transcendentals=0),
    )(*operands, *after)


def turned_terms(rows):
    turned = rows.T
    high = turned.astype(BF16)
    return jnp.concatenate([high, (turned - high.astype(F32)).astype(BF16)], axis=0)


def pool_part(terms, count_rows):
    part = jnp.dot(terms, count_rows, preferred_element_type=F32)
    return part[:E] + part[E:]


def pool_near_kernel(own, other, c0, c1, c2, c3, out):
    a, b = turned_terms(own[...]), turned_terms(other[...])
    for d, c in enumerate((c0, c1, c2, c3)):
        out[d] = pool_part(a, c[:NEAR]) + pool_part(b, c[HALF_ROWS : HALF_ROWS + NEAR])


def pool_far_kernel(own, base, c0, c1, c2, c3, out):
    a = turned_terms(own[...])
    for d, c in enumerate((c0, c1, c2, c3)):
        out[d] = base[d] + pool_part(a, c[NEAR:HALF_ROWS])


def pool_last_kernel(d, other, base, c, out):
    b = turned_terms(other[...])
    total = base[d] + pool_part(b, c[HALF_ROWS + NEAR :])
    for i in range(NX):
        s = slice(i * SB, (i + 1) * SB)
        out[s] = total[:, s].T


def owners_kernel(a, b, c, d, o0, o1, o2, o3):
    for i, out in enumerate((o0, o1, o2, o3)):
        s = slice(i * SB, (i + 1) * SB)
        out[...] = (a[s] + b[s]) + (c[s] + d[s])


def cross_kernel(pos, b0, b1, b2, b3, u, v, bias, cot, crossed, g0, g1, g2, g3, x_ref):
    def columns(d):
        return pl.ds(pl.multiple_of(((pos[0] - d) & (NX - 1)) * E, E), E)

    for d, b in enumerate((b0, b1, b2, b3)):
        x_ref[:, columns(d)] = b[...]
    base_x = x_ref[...]
    low = jnp.dot(base_x.astype(BF16), u[...], preferred_element_type=F32).astype(BF16)
    scale = jnp.dot(low, v[...], preferred_element_type=F32) + bias[...]
    crossed[...] = (base_x * scale + base_x).astype(BF16)
    upstream = cot[...].astype(F32)
    mixed = (upstream * base_x).astype(BF16)
    last = (((1,), (1,)), ((), ()))
    back_low = lax.dot_general(mixed, v[...], last, preferred_element_type=F32).astype(BF16)
    x_ref[...] = upstream * (scale + 1.0) + lax.dot_general(
        back_low, u[...], last, preferred_element_type=F32
    )
    for d, g in enumerate((g0, g1, g2, g3)):
        g[...] = x_ref[:, columns(d)]


def cross(pos, parts, u, v, bias, cot):
    vm = pl.BlockSpec(memory_space=pltpu.VMEM)
    return pl.pallas_call(
        cross_kernel,
        in_specs=[pl.BlockSpec(memory_space=pltpu.SMEM)] + [vm] * 8,
        out_specs=[vm] * 5,
        out_shape=[jax.ShapeDtypeStruct(cot.shape, BF16)] + [jax.ShapeDtypeStruct((SB, E), F32)] * NX,
        scratch_shapes=[pltpu.VMEM(cot.shape, F32)],
        compiler_params=VMEM,
        cost_estimate=pl.CostEstimate(flops=8 * SB * 512 * 512, bytes_accessed=2 << 20, transcendentals=0),
    )(pos, *parts, u, v, bias, cot)


def stack_kernel(a, b, c, d, out):
    for i, ref in enumerate((a, b, c, d)):
        out[i * SB : (i + 1) * SB] = ref[...]


def grad_terms_kernel(g0, g1, g2, g3, c0, c1, c2, c3, out, terms):
    for d, g in enumerate((g0, g1, g2, g3)):
        terms[d] = split_terms(g[...])
    grads_kernel(slice(HALF_ROWS + NEAR, NC * HALF_ROWS), terms, c0, c1, c2, c3, out)


def grads_kernel(rows, terms, c0, c1, c2, c3, *refs):
    out = refs[-1]
    total = None
    for d, c in enumerate((c0, c1, c2, c3)):
        part = jnp.dot(c[rows], terms[d], preferred_element_type=F32)
        total = part if total is None else total + part
    out[...] = total[:, :E] + total[:, E:]


def grads(counts, terms, rows, *after):
    vm = pl.BlockSpec(memory_space=pltpu.VMEM)
    amount = rows.stop - rows.start
    return pl.pallas_call(
        functools.partial(grads_kernel, rows),
        in_specs=[vm] * 5 + [pl.BlockSpec(memory_space=pl.ANY)] * len(after),
        out_specs=vm,
        out_shape=jax.ShapeDtypeStruct((amount, E), F32),
        compiler_params=VMEM,
        cost_estimate=pl.CostEstimate(
            flops=4 * amount * NY * SAMPLES_Y * E, bytes_accessed=1 << 20, transcendentals=0
        ),
    )(terms, *counts, *after)


def far_sums_kernel(a, b, up, down):
    h = RB // 2
    total = a[...] + b[...]
    up[...] = total[: RB + h]
    down[:RB] = total[2 * RB :]
    down[RB:] = total[RB + h : 2 * RB]


def near_sums_kernel(a, b, up, down, keep, p1, p2, m2, m1):
    h = RB // 2
    m2[...] = a[:RB] + b[:RB]
    m2[h:] += down[RB:]
    m1[...] = a[RB : 2 * RB] + b[RB : 2 * RB] + down[:RB]
    keep[...] = a[2 * RB : 3 * RB] + b[2 * RB : 3 * RB]
    p1[...] = a[3 * RB : 4 * RB] + b[3 * RB : 4 * RB] + up[:RB]
    p2[...] = a[4 * RB :] + b[4 * RB :]
    p2[:h] += up[RB:]


def update_kernel(keep, a, b, c, d, rows, accum, new_rows, new_accum):
    grad = keep[...] + ((a[...] + b[...]) + (c[...] + d[...]))
    mean = jnp.sum(grad * grad, axis=1, keepdims=True) * (1.0 / E)
    mean_row = jnp.broadcast_to(mean, (RB, E)).T[:1]
    total = accum[...] + mean_row
    new_accum[...] = total
    total_column = jnp.broadcast_to(total, (E, RB)).T
    new_rows[...] = rows[...] - learn_rate * grad / jnp.sqrt(total_column)


def per_device(
    table_rows, row_accum, row_ids, sketch_bits, cross_u, cross_v, cross_bias, cotangent
):
    pos = jnp.stack([lax.axis_index(a) for a in ("hst", "z", "y", "core")]).astype(jnp.int32)
    own = table_rows[0]

    def by_owner(entries):
        return entries[0].reshape(BAG, -1, SB).transpose(1, 0, 2).reshape(NX, NZ, NY, NC, BAG, SB)

    ids, bits = by_owner(row_ids), by_owner(sketch_bits)
    third = (RB + RB // 2, E)
    p1, m1 = move(own, "z", 1), move(own, "z", -1)
    p2, m2 = move(own, "z", 2), move(own, "z", -2)
    entries = entries_of(pos, ids, bits)
    first = [counts_of(entries, d) for d in (2, 1)]
    near, up, down = call_after(forward_kernel, [(NEAR, E), third, third], (own, p1, m1, p2, m2), first)
    p3, m3 = move(up, "z", 2), move(down, "z", -2)
    other_near = move(near, "core", 1)
    last = [counts_of(entries, d, near) for d in (3, 0)]
    counts = [last[1], first[1], first[0], last[0]]
    turned = (NY, E, SAMPLES_Y)
    bags = call(pool_near_kernel, [(turned, F32)], near, other_near, *counts, flops=1 << 30)[0]
    far = call_after(far_rows_kernel, [(HALF_ROWS - NEAR, E)], (p3, m3), [bags])[0]
    other_far = move(far, "core", 1)
    bags = call(pool_far_kernel, [(turned, F32)], far, bags, *counts, flops=1 << 28)[0]
    pooled = [None] * NY
    for d in (2, 1, 3, 0):
        (pooled[d],) = call(
            functools.partial(pool_last_kernel, d),
            [((SAMPLES_Y, E), F32)],
            other_far,
            bags,
            counts[d],
            flops=1 << 27,
        )
    block = ((SB, E), F32)
    mine = call(
        owners_kernel,
        [block] * NX,
        pooled[0],
        move(pooled[1], "y", 1),
        move(pooled[2], "y", 2),
        move(pooled[3], "y", -1),
    )
    parts = [mine[0]] + [move(mine[d], "hst", d) for d in range(1, NX)]
    crossed, *grad_parts = cross(
        pos, parts, cross_u, cross_v, cross_bias.reshape(1, -1), cotangent
    )
    back = [grad_parts[0]] + [move(grad_parts[d], "hst", -d) for d in range(1, NX)]
    (bag_grads,) = call(stack_kernel, [((SAMPLES_Y, E), F32)], *back)
    all_grads = [bag_grads] + [move(bag_grads, "y", -d) for d in range(1, NY)]
    far_shape = (HALF_ROWS - NEAR, E)
    other_far, terms = call(
        grad_terms_kernel,
        [(far_shape, F32), ((NY, SAMPLES_Y, 2 * E), BF16)],
        *all_grads,
        *counts,
        flops=1 << 29,
    )
    from_far = move(other_far, "core", 1)
    own_far = grads(counts, terms, slice(NEAR, HALF_ROWS))
    up, down = call(far_sums_kernel, [(third, F32)] * 2, own_far, from_far)
    up_in, down_in = move(up, "z", 2), move(down, "z", -2)
    other_near = grads(counts, terms, slice(HALF_ROWS, HALF_ROWS + NEAR), up)
    from_near = move(other_near, "core", 1)
    own_near = grads(counts, terms, slice(0, NEAR), up)
    keep, *near = call(near_sums_kernel, [block] * 5, own_near, from_near, up_in, down_in)
    sums = [move(a, "z", s) for a, s in zip(near, (1, 2, -2, -1))]
    new_rows, new_accum = call(
        update_kernel, [block, ((1, RB), F32)], keep, *sums, own, row_accum
    )
    return (crossed, new_rows[None], new_accum)


def solution(mesh):
    grid = Mesh(mesh.devices.reshape(NX, NZ, NY, NC), ("hst", "z", "y", "core"))
    local = ("z", "y", "core")
    in_specs = (
        P("hst", local, None),
        P("hst", local),
        P("hst", None, None),
        P("hst", None, None),
        P(),
        P(),
        P(),
        P(("hst",) + local, None),
    )
    out_specs = (P(("hst",) + local, None), P("hst", local, None), P("hst", local))
    return jax.shard_map(
        per_device, mesh=grid, in_specs=in_specs, out_specs=out_specs, check_vma=False
    )
```

```python
import functools

import jax
import jax.numpy as jnp
from jax import lax
from jax.experimental import pallas as pl
from jax.experimental.pallas import tpu as pltpu
from jax.sharding import Mesh, PartitionSpec as P

learn_rate = 0.1
NX, NZ, NY, NC = 4, 8, 4, 2
RB, SB, E, BAG = 128, 128, 128, 8
SIZES = {"hst": NX, "z": NZ, "y": NY, "core": NC}
HALF_ROWS = NZ * RB
RADIX = 17
SAMPLES_Y = NX * SB
F32, BF16 = jnp.float32, jnp.bfloat16
VMEM = pltpu.CompilerParams(vmem_limit_bytes=40 << 20)
SMALL = pl.CostEstimate(flops=0, bytes_accessed=1024, transcendentals=0)


def move(array, axis, step):
    n = SIZES[axis]
    return lax.ppermute(array, axis, [(i, (i + step) % n) for i in range(n)])


def move_ways(array, axis, step):
    n = SIZES[axis]
    pairs = [
        (i * NC + c, (i + (step if c == 0 else -step)) % n * NC + c) for i in range(n) for c in range(NC)
    ]
    return lax.ppermute(array, (axis, "core"), pairs)


def call(kernel, out_shapes, *operands):
    vm = pl.BlockSpec(memory_space=pltpu.VMEM)
    return pl.pallas_call(
        kernel,
        in_specs=[vm] * len(operands),
        out_specs=[vm] * len(out_shapes),
        out_shape=[jax.ShapeDtypeStruct(s, d) for s, d in out_shapes],
        compiler_params=VMEM,
        cost_estimate=SMALL,
    )(*operands)


def split_terms(value):
    high = value.astype(BF16)
    return jnp.concatenate([high, (value - high.astype(F32)).astype(BF16)], axis=1)


def entries_kernel(pos, ids, bits, spot_ref, value_ref):
    z, y, c = pos[1], pos[2], pos[3]
    for x in range(NX):
        for at_y in range(NY):
            row = ids[x, at_y, c]
            steps = ((z - (row >> 10)) * (1 - 2 * c)) & (NZ - 1)
            crossed = ((row >> 7) & 1) ^ c
            beyond = steps > NZ // 2
            ends = (steps & (NZ // 2 - 1)) == 0
            other = jnp.where(ends, crossed, jnp.where(beyond, 1, 0))
            near_core = jnp.where(ends, 0, crossed ^ other)
            k = jnp.where(beyond, NZ - steps, steps)
            spot = jnp.where(k == 0, 0, (2 * k - 1 + near_core) * RB) + (row & (RB - 1))
            spot_ref[x, at_y] = jnp.where(((row >> 8) & (NY - 1)) == y, spot, -1)
            value_ref[x, at_y] = (2 * bits[x, at_y, c] - 1).astype(F32) * (1 + (RADIX - 1) * other).astype(F32)


def entries_of(pos, ids, bits):
    shape = (4, NX, BAG, SB)
    vm = pl.BlockSpec(memory_space=pltpu.VMEM)
    return pl.pallas_call(
        entries_kernel,
        in_specs=[pl.BlockSpec(memory_space=pltpu.SMEM), vm, vm],
        out_specs=[vm] * 2,
        out_shape=[jax.ShapeDtypeStruct(shape, jnp.int32), jax.ShapeDtypeStruct(shape, F32)],
        compiler_params=VMEM,
        cost_estimate=SMALL,
    )(pos, ids, bits)


def counts_kernel(spot_ref, value_ref, out_ref):
    rows16 = lax.broadcasted_iota(jnp.int32, (16, SB), 0).astype(jnp.int16)
    for dx in range(NX):
        spots = [jnp.broadcast_to(spot_ref[dx, k : k + 1], (16, SB)).astype(jnp.int16) for k in range(BAG)]
        values = [jnp.broadcast_to(value_ref[dx, k : k + 1], (16, SB)).astype(BF16) for k in range(BAG)]
        columns = slice(dx * SB, (dx + 1) * SB)

        def step(r, carry):
            here = rows16 + (r * 16).astype(jnp.int16)
            terms = [jnp.where(s == here, v, BF16(0)) for s, v in zip(spots, values)]
            while len(terms) > 1:
                terms = [a + b for a, b in zip(terms[::2], terms[1::2])]
            high = (terms[0] * BF16(1.0 / RADIX) + BF16(192)) - BF16(192)
            at = pl.multiple_of(r * 16, 16)
            out_ref[pl.ds(at, 16), columns] = terms[0] - high * BF16(RADIX)
            out_ref[pl.ds(HALF_ROWS + at, 16), columns] = high
            return carry

        lax.fori_loop(0, HALF_ROWS // 16, step, 0, unroll=16)


def counts_of(entries, group, *after):
    vm = pl.BlockSpec(memory_space=pltpu.VMEM)
    spec = pl.BlockSpec((None, NX, BAG, SB), lambda i: (group, 0, 0, 0))
    return pl.pallas_call(
        lambda s, v, *rest: counts_kernel(s, v, rest[-1]),
        grid=(1,),
        in_specs=[spec, spec] + [pl.BlockSpec(memory_space=pl.ANY)] * len(after),
        out_specs=pl.BlockSpec(memory_space=pltpu.VMEM),
        out_shape=jax.ShapeDtypeStruct((NC * HALF_ROWS, SAMPLES_Y), BF16),
        compiler_params=VMEM,
        cost_estimate=SMALL,
    )(*entries, *after)


def pair_kernel(own, other, *refs):
    out, sem = refs[-2:]
    copy = pltpu.make_async_copy(own, out.at[:RB], sem)
    copy.start()
    out[RB:] = other[...]
    copy.wait()


def rows_kernel(own, one, two, three, four, *refs):
    out = refs[-1]
    out[:RB] = own[...]
    for i, ref in enumerate((one, two, three)):
        out[(2 * i + 1) * RB : (2 * i + 3) * RB] = ref[...]
    out[7 * RB :] = four[...]


def call_after(kernel, out_shapes, operands, after, first=pltpu.VMEM, scratch=()):
    vm, anywhere = pl.BlockSpec(memory_space=pltpu.VMEM), pl.BlockSpec(memory_space=pl.ANY)
    return pl.pallas_call(
        kernel,
        in_specs=[pl.BlockSpec(memory_space=first)] + [vm] * (len(operands) - 1) + [anywhere] * len(after),
        out_specs=[vm] * len(out_shapes),
        out_shape=[jax.ShapeDtypeStruct(s, F32) for s in out_shapes],
        scratch_shapes=scratch,
        compiler_params=VMEM,
        cost_estimate=SMALL,
    )(*operands, *after)


def turned_terms(rows):
    turned = rows.T
    high = turned.astype(BF16)
    return jnp.concatenate([high, (turned - high.astype(F32)).astype(BF16)], axis=0)


def pool_part(terms, count_rows):
    part = jnp.dot(terms, count_rows, preferred_element_type=F32)
    return part[:E] + part[E:]


def pool_own_kernel(rows, c0, c1, c2, c3, out):
    terms = turned_terms(rows[...])
    for x, c in enumerate((c0, c1, c2, c3)):
        out[x] = pool_part(terms, c[:HALF_ROWS])


def pool_other_kernel(rows, base, c0, c1, c2, c3, out):
    terms = turned_terms(rows[...])
    for x, c in enumerate((c0, c1, c2, c3)):
        total = base[x] + pool_part(terms, c[HALF_ROWS:])
        for y in range(NY):
            out[x * NY + y] = total[:, y * SB : (y + 1) * SB].T


def cross_kernel(parts, u, v, bias, cot, crossed, out):
    x = [sum(parts[t * NY + y] for y in range(1, NY)) + parts[t * NY] for t in range(NX)]
    base_x = jnp.concatenate(x, axis=1)
    low = jnp.dot(base_x.astype(BF16), u[...], preferred_element_type=F32).astype(BF16)
    scale = jnp.dot(low, v[...], preferred_element_type=F32) + bias[...]
    crossed[...] = (base_x * scale + base_x).astype(BF16)
    upstream = cot[...].astype(F32)
    mixed = (upstream * base_x).astype(BF16)
    last = (((1,), (1,)), ((), ()))
    back_low = lax.dot_general(mixed, v[...], last, preferred_element_type=F32).astype(BF16)
    grad_x = upstream * (scale + 1.0) + lax.dot_general(
        back_low, u[...], last, preferred_element_type=F32
    )
    for t in range(NX):
        for y in range(NY):
            out[t * NY + y] = grad_x[:, t * E : (t + 1) * E]


def rows_grads(rows, terms, counts):
    total = None
    for x, c in enumerate(counts):
        part = jnp.dot(c[rows], terms[x], preferred_element_type=F32)
        total = part if total is None else total + part
    return total[:, :E] + total[:, E:]


def other_grads_kernel(g, c0, c1, c2, c3, out, terms):
    for x in range(NX):
        terms[x] = split_terms(g[x * SAMPLES_Y : (x + 1) * SAMPLES_Y])
    out[...] = rows_grads(slice(HALF_ROWS, NC * HALF_ROWS), terms, (c0, c1, c2, c3))


def own_grads_kernel(terms, c0, c1, c2, c3, out):
    out[...] = rows_grads(slice(0, HALF_ROWS), terms, (c0, c1, c2, c3))


def sums_kernel(a, b, keep, one, two, three, four):
    keep[...] = a[:RB] + b[:RB]
    for i, ref in enumerate((one, two, three)):
        s = slice((2 * i + 1) * RB, (2 * i + 3) * RB)
        ref[...] = a[s] + b[s]
    four[...] = a[7 * RB :] + b[7 * RB :]


def last_sums_kernel(keep, one, two, three, four, mine, other):
    mine[...] = (keep[...] + four[...]) + (one[:RB] + two[:RB] + three[:RB])
    other[...] = one[RB:] + two[RB:] + three[RB:]


def update_kernel(a, b, rows, accum, new_rows, new_accum):
    grad = a[...] + b[...]
    mean = jnp.sum(grad * grad, axis=1, keepdims=True) * (1.0 / E)
    mean_row = jnp.broadcast_to(mean, (RB, E)).T[:1]
    total = accum[...] + mean_row
    new_accum[...] = total
    total_column = jnp.broadcast_to(total, (E, RB)).T
    new_rows[...] = rows[...] - learn_rate * grad / jnp.sqrt(total_column)


def per_device(
    table_rows, row_accum, row_ids, sketch_bits, cross_u, cross_v, cross_bias, cotangent
):
    pos = jnp.stack([lax.axis_index(a) for a in ("hst", "z", "y", "core")]).astype(jnp.int32)
    own = table_rows[0]

    def at_own_z(entries):
        by_owner = entries[0].reshape(BAG, -1, SB).transpose(1, 0, 2).reshape(NX, NZ, NY, NC, BAG, SB)
        return lax.dynamic_index_in_dim(by_owner, pos[1], 1, keepdims=False)

    ids, bits = at_own_z(row_ids), at_own_z(sketch_bits)
    other = move(own, "core", 1)
    (pair,) = call_after(
        pair_kernel, [(2 * RB, E)], (own, other), (), pl.ANY, [pltpu.SemaphoreType.DMA]
    )
    four, three = move_ways(own, "z", 4), move_ways(pair, "z", 3)
    two, one = move_ways(pair, "z", 2), move_ways(pair, "z", 1)
    entries = entries_of(pos, ids, bits)
    counts = [counts_of(entries, x) for x in range(NX)]
    (rows,) = call_after(rows_kernel, [(HALF_ROWS, E)], (own, one, two, three, four), counts)
    other_rows = move(rows, "core", 1)
    (bags,) = call(pool_own_kernel, [((NX, E, SAMPLES_Y), F32)], rows, *counts)
    blocks = ((NX * NY, SB, E), F32)
    (bags,) = call(pool_other_kernel, [blocks], other_rows, bags, *counts)

    def exchange(parts):
        return lax.all_to_all(parts, ("hst", "y"), split_axis=0, concat_axis=0, tiled=True)

    crossed, bag_grads = call(
        cross_kernel,
        [(cotangent.shape, BF16), blocks],
        exchange(bags),
        cross_u,
        cross_v,
        cross_bias.reshape(1, -1),
        cotangent,
    )
    bag_grads = exchange(bag_grads).reshape(NX * NY * SB, E)
    block, pair, half = (((n * RB, E), F32) for n in (1, 2, 8))
    terms_shape = ((NX, SAMPLES_Y, 2 * E), BF16)
    other_grads, terms = call(other_grads_kernel, [half, terms_shape], bag_grads, *counts)
    from_core = move(other_grads, "core", 1)
    (own_grads,) = call(own_grads_kernel, [half], terms, *counts)
    keep, *sums = call(sums_kernel, [block, pair, pair, pair, block], own_grads, from_core)
    far = [move_ways(sums[s - 1], "z", -s) for s in (4, 3, 2, 1)]
    mine, others = call(last_sums_kernel, [block] * 2, keep, *far[::-1])
    new_rows, new_accum = call(
        update_kernel, [block, ((1, RB), F32)], mine, move(others, "core", 1), own, row_accum
    )
    return (crossed, new_rows[None], new_accum)


def solution(mesh):
    grid = Mesh(mesh.devices.reshape(NX, NZ, NY, NC), ("hst", "z", "y", "core"))
    local = ("z", "y", "core")
    in_specs = (
        P("hst", local, None),
        P("hst", local),
        P("hst", None, None),
        P("hst", None, None),
        P(),
        P(),
        P(),
        P(("hst",) + local, None),
    )
    out_specs = (P(("hst",) + local, None), P("hst", local, None), P("hst", local))
    return jax.shard_map(
        per_device, mesh=grid, in_specs=in_specs, out_specs=out_specs, check_vma=False
    )
```

```python
import functools

import jax
import jax.numpy as jnp
from jax import lax
from jax.experimental import pallas as pl
from jax.experimental.pallas import tpu as pltpu
from jax.sharding import Mesh, PartitionSpec as P

learn_rate = 0.1
NX, NZ, NY, NC = 4, 8, 4, 2
RB, SB, E, BAG = 128, 128, 128, 8
SIZES = {"hst": NX, "z": NZ, "y": NY, "core": NC}
HALF_ROWS = NZ * RB
RADIX = 17
SAMPLES_Y = NX * SB
F32, BF16 = jnp.float32, jnp.bfloat16
VMEM = pltpu.CompilerParams(vmem_limit_bytes=40 << 20)
SMALL = pl.CostEstimate(flops=0, bytes_accessed=1024, transcendentals=0)


def move(array, axis, step):
    n = SIZES[axis]
    return lax.ppermute(array, axis, [(i, (i + step) % n) for i in range(n)])


def move_ways(array, axis, step):
    n = SIZES[axis]
    pairs = [
        (i * NC + c, (i + (step if c == 0 else -step)) % n * NC + c) for i in range(n) for c in range(NC)
    ]
    return lax.ppermute(array, (axis, "core"), pairs)


def call(kernel, out_shapes, *operands):
    vm = pl.BlockSpec(memory_space=pltpu.VMEM)
    return pl.pallas_call(
        kernel,
        in_specs=[vm] * len(operands),
        out_specs=[vm] * len(out_shapes),
        out_shape=[jax.ShapeDtypeStruct(s, d) for s, d in out_shapes],
        compiler_params=VMEM,
        cost_estimate=SMALL,
    )(*operands)


def split_terms(value):
    high = value.astype(BF16)
    return jnp.concatenate([high, (value - high.astype(F32)).astype(BF16)], axis=1)


def entries_of(row_ids, sketch_bits):
    z, y, c = (lax.axis_index(a).astype(jnp.int32) for a in ("z", "y", "core"))

    def at_own(entries):
        by_owner = entries[0].reshape(BAG, -1, SB).transpose(1, 0, 2).reshape(NX, NZ, NY, NC, BAG, SB)
        part = lax.dynamic_slice(by_owner, (0, z, 0, c, 0, 0), (NX, 1, NY, 1, BAG, SB))
        return part.reshape(NX, NY, BAG, SB)

    row, bits = at_own(row_ids), at_own(sketch_bits)
    steps = ((z - (row >> 10)) * (1 - 2 * c)) & (NZ - 1)
    crossed = ((row >> 7) & 1) ^ c
    beyond = steps > NZ // 2
    ends = (steps & (NZ // 2 - 1)) == 0
    other = jnp.where(ends, crossed, beyond.astype(jnp.int32))
    near_core = jnp.where(ends, 0, crossed ^ other)
    k = jnp.where(beyond, NZ - steps, steps)
    spot = jnp.where(k == 0, 0, (2 * k - 1 + near_core) * RB) + (row & (RB - 1))
    spot = jnp.where(((row >> 8) & (NY - 1)) == y, spot, -1)
    return spot, ((2 * bits - 1) * (1 + (RADIX - 1) * other)).astype(F32)


def counts_kernel(spot_ref, value_ref, out_ref):
    rows16 = lax.broadcasted_iota(jnp.int32, (16, SB), 0).astype(jnp.int16)
    for dx in range(NX):
        spots = [jnp.broadcast_to(spot_ref[dx, k : k + 1], (16, SB)).astype(jnp.int16) for k in range(BAG)]
        values = [jnp.broadcast_to(value_ref[dx, k : k + 1], (16, SB)).astype(BF16) for k in range(BAG)]
        columns = slice(dx * SB, (dx + 1) * SB)

        def step(r, carry):
            here = rows16 + (r * 16).astype(jnp.int16)
            terms = [jnp.where(s == here, v, BF16(0)) for s, v in zip(spots, values)]
            while len(terms) > 1:
                terms = [a + b for a, b in zip(terms[::2], terms[1::2])]
            high = (terms[0] * BF16(1.0 / RADIX) + BF16(192)) - BF16(192)
            at = pl.multiple_of(r * 16, 16)
            out_ref[pl.ds(at, 16), columns] = terms[0] - high * BF16(RADIX)
            out_ref[pl.ds(HALF_ROWS + at, 16), columns] = high
            return carry

        lax.fori_loop(0, HALF_ROWS // 16, step, 0, unroll=16)


def counts_of(entries, group, *after):
    vm = pl.BlockSpec(memory_space=pltpu.VMEM)
    spec = pl.BlockSpec((None, NX, BAG, SB), lambda i: (group, 0, 0, 0))
    return pl.pallas_call(
        lambda s, v, *rest: counts_kernel(s, v, rest[-1]),
        grid=(1,),
        in_specs=[spec, spec] + [pl.BlockSpec(memory_space=pl.ANY)] * len(after),
        out_specs=pl.BlockSpec(memory_space=pltpu.VMEM),
        out_shape=jax.ShapeDtypeStruct((NC * HALF_ROWS, SAMPLES_Y), BF16),
        compiler_params=VMEM,
        cost_estimate=SMALL,
    )(*entries, *after)


def copy_kernel(a, *refs):
    refs[-1][...] = a[...]


def pair_kernel(own, other, out):
    out[:RB] = own[...]
    out[RB:] = other[...]


def onward_kernel(three, *refs):
    refs[-1][...] = three[:RB]


def rows_kernel(pair, one, two, three, four, *refs):
    out = refs[-1]
    out[:RB] = pair[:RB]
    for i, ref in enumerate((one, two, three)):
        out[(2 * i + 1) * RB : (2 * i + 3) * RB] = ref[...]
    out[7 * RB :] = four[...]


def call_after(kernel, out_shapes, operands, after):
    vm, anywhere = pl.BlockSpec(memory_space=pltpu.VMEM), pl.BlockSpec(memory_space=pl.ANY)
    return pl.pallas_call(
        kernel,
        in_specs=[vm] * len(operands) + [anywhere] * len(after),
        out_specs=[vm] * len(out_shapes),
        out_shape=[jax.ShapeDtypeStruct(s, F32) for s in out_shapes],
        compiler_params=VMEM,
        cost_estimate=SMALL,
    )(*operands, *after)


def turned_terms(rows):
    turned = rows.T
    high = turned.astype(BF16)
    return jnp.concatenate([high, (turned - high.astype(F32)).astype(BF16)], axis=0)


def pool_part(terms, count_rows):
    part = jnp.dot(terms, count_rows, preferred_element_type=F32)
    return part[:E] + part[E:]


def pool_own_kernel(rows, c0, c1, c2, c3, out):
    terms = turned_terms(rows[...])
    for x, c in enumerate((c0, c1, c2, c3)):
        out[x] = pool_part(terms, c[:HALF_ROWS])


def pool_other_kernel(rows, base, c0, c1, c2, c3, out):
    terms = turned_terms(rows[...])
    for x, c in enumerate((c0, c1, c2, c3)):
        total = base[x] + pool_part(terms, c[HALF_ROWS:])
        for y in range(NY):
            out[x * NY + y] = total[:, y * SB : (y + 1) * SB].T


def cross_kernel(parts, u, v, bias, cot, crossed, out):
    x = [sum(parts[t * NY + y] for y in range(1, NY)) + parts[t * NY] for t in range(NX)]
    base_x = jnp.concatenate(x, axis=1)
    low = jnp.dot(base_x.astype(BF16), u[...], preferred_element_type=F32).astype(BF16)
    scale = jnp.dot(low, v[...], preferred_element_type=F32) + bias[...]
    crossed[...] = (base_x * scale + base_x).astype(BF16)
    upstream = cot[...].astype(F32)
    mixed = (upstream * base_x).astype(BF16)
    last = (((1,), (1,)), ((), ()))
    back_low = lax.dot_general(mixed, v[...], last, preferred_element_type=F32).astype(BF16)
    grad_x = upstream * (scale + 1.0) + lax.dot_general(
        back_low, u[...], last, preferred_element_type=F32
    )
    for t in range(NX):
        for y in range(NY):
            out[t * NY + y] = grad_x[:, t * E : (t + 1) * E]


def rows_grads(rows, terms, counts):
    total = None
    for x, c in enumerate(counts):
        part = jnp.dot(c[rows], terms[x], preferred_element_type=F32)
        total = part if total is None else total + part
    return total[:, :E] + total[:, E:]


def other_grads_kernel(g, c0, c1, c2, c3, out, terms):
    for x in range(NX):
        terms[x] = split_terms(g[x * SAMPLES_Y : (x + 1) * SAMPLES_Y])
    out[...] = rows_grads(slice(HALF_ROWS, NC * HALF_ROWS), terms, (c0, c1, c2, c3))


def own_grads_kernel(terms, c0, c1, c2, c3, out):
    out[...] = rows_grads(slice(0, HALF_ROWS), terms, (c0, c1, c2, c3))


def sums_kernel(a, b, four, two, one, three, keep):
    keep[...] = a[:RB] + b[:RB]
    for i, ref in enumerate((one, two, three)):
        s = slice((2 * i + 1) * RB, (2 * i + 3) * RB)
        ref[...] = a[s] + b[s]
    four[...] = a[7 * RB :] + b[7 * RB :]


def relay_kernel(three, four, out):
    out[:RB] = three[:RB] + four[...]
    out[RB:] = three[RB:]


def last_sums_kernel(three, two, one, keep, mine, other):
    mine[...] = keep[...] + (one[:RB] + two[:RB] + three[:RB])
    other[...] = one[RB:] + two[RB:] + three[RB:]


def update_kernel(a, b, rows, accum, new_rows, new_accum):
    grad = a[...] + b[...]
    mean = jnp.sum(grad * grad, axis=1, keepdims=True) * (1.0 / E)
    mean_row = jnp.broadcast_to(mean, (RB, E)).T[:1]
    total = accum[...] + mean_row
    new_accum[...] = total
    total_column = jnp.broadcast_to(total, (E, RB)).T
    new_rows[...] = rows[:RB] - learn_rate * grad / jnp.sqrt(total_column)


def per_device(
    table_rows, row_accum, row_ids, sketch_bits, cross_u, cross_v, cross_bias, cotangent
):
    own = table_rows[0]

    other = move(own, "core", 1)
    (held,) = call(copy_kernel, [((RB, E), F32)], own)
    (pair,) = call(pair_kernel, [((2 * RB, E), F32)], held, other)
    three, two, one = (move_ways(pair, "z", s) for s in (3, 2, 1))
    entries = entries_of(row_ids, sketch_bits)
    counts = [counts_of(entries, x) for x in range(2)]
    (onward,) = call_after(onward_kernel, [(RB, E)], (three,), counts)
    four = move_ways(onward, "z", 1)
    counts = counts + [counts_of(entries, x, onward) for x in range(2, NX)]
    (rows,) = call_after(rows_kernel, [(HALF_ROWS, E)], (pair, one, two, three, four), counts)
    other_rows = move(rows, "core", 1)
    (bags,) = call(pool_own_kernel, [((NX, E, SAMPLES_Y), F32)], rows, *counts)
    blocks = ((NX * NY, SB, E), F32)
    (bags,) = call(pool_other_kernel, [blocks], other_rows, bags, *counts)

    def exchange(parts):
        return lax.all_to_all(parts, ("hst", "y"), split_axis=0, concat_axis=0, tiled=True)

    crossed, bag_grads = call(
        cross_kernel,
        [(cotangent.shape, BF16), blocks],
        exchange(bags),
        cross_u,
        cross_v,
        cross_bias.reshape(1, -1),
        cotangent,
    )
    bag_grads = exchange(bag_grads).reshape(NX * NY * SB, E)
    block, pair_shape, half = (((n * RB, E), F32) for n in (1, 2, 8))
    terms_shape = ((NX, SAMPLES_Y, 2 * E), BF16)
    other_grads, terms = call(other_grads_kernel, [half, terms_shape], bag_grads, *counts)
    from_core = move(other_grads, "core", 1)
    (own_grads,) = call(own_grads_kernel, [half], terms, *counts)
    four, two, one, three, keep = call(
        sums_kernel, [block, pair_shape, pair_shape, pair_shape, block], own_grads, from_core
    )
    four_in, two_in, one_in = (move_ways(v, "z", -s) for v, s in ((four, 1), (two, 2), (one, 1)))
    (three,) = call(relay_kernel, [pair_shape], three, four_in)
    three_in = move_ways(three, "z", -3)
    mine, others = call(last_sums_kernel, [block] * 2, three_in, two_in, one_in, keep)
    new_rows, new_accum = call(
        update_kernel, [block, ((1, RB), F32)], mine, move(others, "core", 1), pair, row_accum
    )
    return (crossed, new_rows[None], new_accum)


def solution(mesh):
    grid = Mesh(mesh.devices.reshape(NX, NZ, NY, NC), ("hst", "z", "y", "core"))
    local = ("z", "y", "core")
    in_specs = (
        P("hst", local, None),
        P("hst", local),
        P("hst", None, None),
        P("hst", None, None),
        P(),
        P(),
        P(),
        P(("hst",) + local, None),
    )
    out_specs = (P(("hst",) + local, None), P("hst", local, None), P("hst", local))
    return jax.shard_map(
        per_device, mesh=grid, in_specs=in_specs, out_specs=out_specs, check_vma=False
    )
```

```python
import functools

import jax
import jax.numpy as jnp
from jax import lax
from jax.experimental import pallas as pl
from jax.experimental.pallas import tpu as pltpu
from jax.sharding import Mesh, PartitionSpec as P

learn_rate = 0.1
NX, NZ, NY, NC = 4, 8, 4, 2
RB, SB, E, BAG = 128, 128, 128, 8
SIZES = {"hst": NX, "z": NZ, "y": NY, "core": NC}
HALF_ROWS = NZ * RB
RADIX = 17
FLIP = 10
SAMPLES_Y = NX * SB
F32, BF16 = jnp.float32, jnp.bfloat16
VMEM = pltpu.CompilerParams(vmem_limit_bytes=40 << 20)
SMALL = pl.CostEstimate(flops=0, bytes_accessed=1024, transcendentals=0)


def move(array, axis, step):
    n = SIZES[axis]
    return lax.ppermute(array, axis, [(i, (i + step) % n) for i in range(n)])


def move_ways(array, axis, step):
    n = SIZES[axis]
    pairs = [
        (i * NC + c, (i + (step if c == 0 else -step)) % n * NC + c) for i in range(n) for c in range(NC)
    ]
    return lax.ppermute(array, (axis, "core"), pairs)


def call(kernel, out_shapes, *operands):
    vm = pl.BlockSpec(memory_space=pltpu.VMEM)
    return pl.pallas_call(
        kernel,
        in_specs=[vm] * len(operands),
        out_specs=[vm] * len(out_shapes),
        out_shape=[jax.ShapeDtypeStruct(s, d) for s, d in out_shapes],
        compiler_params=VMEM,
        cost_estimate=SMALL,
    )(*operands)


def own_flip():
    return lax.axis_index("core").astype(jnp.int32) * FLIP


def exchange(parts):
    groups = []
    for z in range(NZ):
        for c in range(NC):
            places = [place ^ (FLIP * c) for place in range(NX * NY)]
            groups.append([((p // NY * NZ + z) * NY + p % NY) * NC + c for p in places])
    return lax.all_to_all(
        parts, ("hst", "z", "y", "core"), split_axis=0, concat_axis=0, tiled=True, axis_index_groups=groups
    )


def split_terms(value):
    high = value.astype(BF16)
    return jnp.concatenate([high, (value - high.astype(F32)).astype(BF16)], axis=1)


def entries_of(row_ids, sketch_bits):
    z, y, c = (lax.axis_index(a).astype(jnp.int32) for a in ("z", "y", "core"))

    def at_own(entries):
        by_owner = entries[0].reshape(BAG, -1, SB).transpose(1, 0, 2).reshape(NX, NZ, NY, NC, BAG, SB)
        part = lax.dynamic_slice(by_owner, (0, z, 0, c, 0, 0), (NX, 1, NY, 1, BAG, SB))
        return part.reshape(NX, NY, BAG, SB)

    row, bits = at_own(row_ids), at_own(sketch_bits)
    steps = ((z - (row >> 10)) * (1 - 2 * c)) & (NZ - 1)
    crossed = ((row >> 7) & 1) ^ c
    beyond = steps > NZ // 2
    ends = (steps & (NZ // 2 - 1)) == 0
    other = jnp.where(ends, crossed, beyond.astype(jnp.int32))
    near_core = jnp.where(ends, 0, crossed ^ other)
    k = jnp.where(beyond, NZ - steps, steps)
    spot = jnp.where(k == 0, 0, (2 * k - 1 + near_core) * RB) + (row & (RB - 1))
    spot = jnp.where(((row >> 8) & (NY - 1)) == y, spot, -1)
    return spot, ((2 * bits - 1) * (1 + (RADIX - 1) * other)).astype(F32)


def counts_kernel(spot_ref, value_ref, out_ref):
    rows16 = lax.broadcasted_iota(jnp.int32, (16, SB), 0).astype(jnp.int16)
    for dx in range(NX):
        spots = [jnp.broadcast_to(spot_ref[dx, k : k + 1], (16, SB)).astype(jnp.int16) for k in range(BAG)]
        values = [jnp.broadcast_to(value_ref[dx, k : k + 1], (16, SB)).astype(BF16) for k in range(BAG)]
        columns = slice(dx * SB, (dx + 1) * SB)

        def step(r, carry):
            here = rows16 + (r * 16).astype(jnp.int16)
            terms = [jnp.where(s == here, v, BF16(0)) for s, v in zip(spots, values)]
            while len(terms) > 1:
                terms = [a + b for a, b in zip(terms[::2], terms[1::2])]
            high = (terms[0] * BF16(1.0 / RADIX) + BF16(192)) - BF16(192)
            at = pl.multiple_of(r * 16, 16)
            out_ref[pl.ds(at, 16), columns] = terms[0] - high * BF16(RADIX)
            out_ref[pl.ds(HALF_ROWS + at, 16), columns] = high
            return carry

        lax.fori_loop(0, HALF_ROWS // 16, step, 0, unroll=16)


def counts_of(entries, group, *after):
    vm = pl.BlockSpec(memory_space=pltpu.VMEM)
    spec = pl.BlockSpec((None, NX, BAG, SB), lambda i: (group, 0, 0, 0))
    return pl.pallas_call(
        lambda s, v, *rest: counts_kernel(s, v, rest[-1]),
        grid=(1,),
        in_specs=[spec, spec] + [pl.BlockSpec(memory_space=pl.ANY)] * len(after),
        out_specs=pl.BlockSpec(memory_space=pltpu.VMEM),
        out_shape=jax.ShapeDtypeStruct((NC * HALF_ROWS, SAMPLES_Y), BF16),
        compiler_params=VMEM,
        cost_estimate=SMALL,
    )(*entries, *after)


def copy_kernel(a, *refs):
    refs[-1][...] = a[...]


def pair_kernel(own, other, out):
    out[:RB] = own[...]
    out[RB:] = other[...]


def onward_kernel(three, *refs):
    refs[-1][...] = three[:RB]


def rows_kernel(pair, one, two, three, four, *refs):
    out = refs[-1]
    out[:RB] = pair[:RB]
    for i, ref in enumerate((one, two, three)):
        out[(2 * i + 1) * RB : (2 * i + 3) * RB] = ref[...]
    out[7 * RB :] = four[...]


def call_after(kernel, out_shapes, operands, after):
    vm, anywhere = pl.BlockSpec(memory_space=pltpu.VMEM), pl.BlockSpec(memory_space=pl.ANY)
    return pl.pallas_call(
        kernel,
        in_specs=[vm] * len(operands) + [anywhere] * len(after),
        out_specs=[vm] * len(out_shapes),
        out_shape=[jax.ShapeDtypeStruct(s, F32) for s in out_shapes],
        compiler_params=VMEM,
        cost_estimate=SMALL,
    )(*operands, *after)


def turned_terms(rows):
    turned = rows.T
    high = turned.astype(BF16)
    return jnp.concatenate([high, (turned - high.astype(F32)).astype(BF16)], axis=0)


def pool_part(terms, count_rows):
    part = jnp.dot(terms, count_rows, preferred_element_type=F32)
    return part[:E] + part[E:]


def pool_own_kernel(rows, c0, c1, c2, c3, out):
    terms = turned_terms(rows[...])
    for x, c in enumerate((c0, c1, c2, c3)):
        out[x] = pool_part(terms, c[:HALF_ROWS])


def pool_other_kernel(rows, base, c0, c1, c2, c3, out):
    flip = own_flip()
    terms = turned_terms(rows[...])
    for x, c in enumerate((c0, c1, c2, c3)):
        total = base[x] + pool_part(terms, c[HALF_ROWS:])
        for y in range(NY):
            out[(x * NY + y) ^ flip] = total[:, y * SB : (y + 1) * SB].T


def cross_kernel(parts, u, v, bias, cot, crossed, out):
    flip = own_flip()
    x = [sum(parts[(t * NY + y) ^ flip] for y in range(1, NY)) + parts[(t * NY) ^ flip] for t in range(NX)]
    base_x = jnp.concatenate(x, axis=1)
    low = jnp.dot(base_x.astype(BF16), u[...], preferred_element_type=F32).astype(BF16)
    scale = jnp.dot(low, v[...], preferred_element_type=F32) + bias[...]
    crossed[...] = (base_x * scale + base_x).astype(BF16)
    upstream = cot[...].astype(F32)
    mixed = (upstream * base_x).astype(BF16)
    last = (((1,), (1,)), ((), ()))
    back_low = lax.dot_general(mixed, v[...], last, preferred_element_type=F32).astype(BF16)
    grad_x = upstream * (scale + 1.0) + lax.dot_general(
        back_low, u[...], last, preferred_element_type=F32
    )
    for t in range(NX):
        for y in range(NY):
            out[(t * NY + y) ^ flip] = grad_x[:, t * E : (t + 1) * E]


def rows_grads(rows, terms, counts):
    total = None
    for x, c in enumerate(counts):
        part = jnp.dot(c[rows], terms[x], preferred_element_type=F32)
        total = part if total is None else total + part
    return total[:, :E] + total[:, E:]


def other_grads_kernel(g, c0, c1, c2, c3, out, terms):
    flip = own_flip()
    for x in range(NX):
        for y in range(NY):
            terms[x, y * SB : (y + 1) * SB] = split_terms(g[(x * NY + y) ^ flip])
    out[...] = rows_grads(slice(HALF_ROWS, NC * HALF_ROWS), terms, (c0, c1, c2, c3))


def own_grads_kernel(terms, c0, c1, c2, c3, out):
    out[...] = rows_grads(slice(0, HALF_ROWS), terms, (c0, c1, c2, c3))


def sums_kernel(a, b, four, two, one, three, keep):
    keep[...] = a[:RB] + b[:RB]
    for i, ref in enumerate((one, two, three)):
        s = slice((2 * i + 1) * RB, (2 * i + 3) * RB)
        ref[...] = a[s] + b[s]
    four[...] = a[7 * RB :] + b[7 * RB :]


def relay_kernel(three, four, out):
    out[:RB] = three[:RB] + four[...]
    out[RB:] = three[RB:]


def last_sums_kernel(three, two, one, keep, mine, other):
    mine[...] = keep[...] + (one[:RB] + two[:RB] + three[:RB])
    other[...] = one[RB:] + two[RB:] + three[RB:]


def update_kernel(a, b, rows, accum, new_rows, new_accum):
    grad = a[...] + b[...]
    mean = jnp.sum(grad * grad, axis=1, keepdims=True) * (1.0 / E)
    mean_row = jnp.broadcast_to(mean, (RB, E)).T[:1]
    total = accum[...] + mean_row
    new_accum[...] = total
    total_column = jnp.broadcast_to(total, (E, RB)).T
    new_rows[...] = rows[:RB] - learn_rate * grad / jnp.sqrt(total_column)


def per_device(
    table_rows, row_accum, row_ids, sketch_bits, cross_u, cross_v, cross_bias, cotangent
):
    own = table_rows[0]

    other = move(own, "core", 1)
    (held,) = call(copy_kernel, [((RB, E), F32)], own)
    (pair,) = call(pair_kernel, [((2 * RB, E), F32)], held, other)
    three, two, one = (move_ways(pair, "z", s) for s in (3, 2, 1))
    entries = entries_of(row_ids, sketch_bits)
    counts = [counts_of(entries, x) for x in range(2)]
    (onward,) = call_after(onward_kernel, [(RB, E)], (three,), counts)
    four = move_ways(onward, "z", 1)
    counts = counts + [counts_of(entries, x, onward) for x in range(2, NX)]
    (rows,) = call_after(rows_kernel, [(HALF_ROWS, E)], (pair, one, two, three, four), counts)
    other_rows = move(rows, "core", 1)
    (bags,) = call(pool_own_kernel, [((NX, E, SAMPLES_Y), F32)], rows, *counts)
    blocks = ((NX * NY, SB, E), F32)
    (bags,) = call(pool_other_kernel, [blocks], other_rows, bags, *counts)

    crossed, bag_grads = call(
        cross_kernel,
        [(cotangent.shape, BF16), blocks],
        exchange(bags),
        cross_u,
        cross_v,
        cross_bias.reshape(1, -1),
        cotangent,
    )
    bag_grads = exchange(bag_grads)
    block, pair_shape, half = (((n * RB, E), F32) for n in (1, 2, 8))
    terms_shape = ((NX, SAMPLES_Y, 2 * E), BF16)
    other_grads, terms = call(
        other_grads_kernel, [half, terms_shape], bag_grads, *counts
    )
    from_core = move(other_grads, "core", 1)
    (own_grads,) = call(own_grads_kernel, [half], terms, *counts)
    four, two, one, three, keep = call(
        sums_kernel, [block, pair_shape, pair_shape, pair_shape, block], own_grads, from_core
    )
    four_in, two_in, one_in = (move_ways(v, "z", -s) for v, s in ((four, 1), (two, 2), (one, 1)))
    (three,) = call(relay_kernel, [pair_shape], three, four_in)
    three_in = move_ways(three, "z", -3)
    mine, others = call(last_sums_kernel, [block] * 2, three_in, two_in, one_in, keep)
    new_rows, new_accum = call(
        update_kernel, [block, ((1, RB), F32)], mine, move(others, "core", 1), pair, row_accum
    )
    return (crossed, new_rows[None], new_accum)


def solution(mesh):
    grid = Mesh(mesh.devices.reshape(NX, NZ, NY, NC), ("hst", "z", "y", "core"))
    local = ("z", "y", "core")
    in_specs = (
        P("hst", local, None),
        P("hst", local),
        P("hst", None, None),
        P("hst", None, None),
        P(),
        P(),
        P(),
        P(("hst",) + local, None),
    )
    out_specs = (P(("hst",) + local, None), P("hst", local, None), P("hst", local))
    return jax.shard_map(
        per_device, mesh=grid, in_specs=in_specs, out_specs=out_specs, check_vma=False
    )
```

```python
import functools

import jax
import jax.numpy as jnp
from jax import lax
from jax.experimental import pallas as pl
from jax.experimental.pallas import tpu as pltpu
from jax.sharding import Mesh, PartitionSpec as P

learn_rate = 0.1
NX, NZ, NY, NC = 4, 8, 4, 2
RB, SB, E, BAG = 128, 128, 128, 8
SIZES = {"hst": NX, "z": NZ, "y": NY, "core": NC}
HALF_ROWS = NZ * RB
RADIX = 17
FLIP = 10
SAMPLES_Y = NX * SB
F32, BF16 = jnp.float32, jnp.bfloat16
VMEM = pltpu.CompilerParams(vmem_limit_bytes=40 << 20)
SMALL = pl.CostEstimate(flops=0, bytes_accessed=1024, transcendentals=0)


def move(array, axis, step):
    n = SIZES[axis]
    return lax.ppermute(array, axis, [(i, (i + step) % n) for i in range(n)])


def move_ways(array, axis, step):
    n = SIZES[axis]
    pairs = [
        (i * NC + c, (i + (step if c == 0 else -step)) % n * NC + c) for i in range(n) for c in range(NC)
    ]
    return lax.ppermute(array, (axis, "core"), pairs)


def call(kernel, out_shapes, *operands):
    vm = pl.BlockSpec(memory_space=pltpu.VMEM)
    return pl.pallas_call(
        kernel,
        in_specs=[vm] * len(operands),
        out_specs=[vm] * len(out_shapes),
        out_shape=[jax.ShapeDtypeStruct(s, d) for s, d in out_shapes],
        compiler_params=VMEM,
        cost_estimate=SMALL,
    )(*operands)


def own_flip():
    return lax.axis_index("core").astype(jnp.int32) * FLIP


def exchange(parts):
    groups = []
    for z in range(NZ):
        for c in range(NC):
            places = [place ^ (FLIP * c) for place in range(NX * NY)]
            groups.append([((p % NX * NZ + z) * NY + p // NX) * NC + c for p in places])
    return lax.all_to_all(
        parts, ("hst", "z", "y", "core"), split_axis=0, concat_axis=0, tiled=True, axis_index_groups=groups
    )


def split_terms(value):
    high = value.astype(BF16)
    return jnp.concatenate([high, (value - high.astype(F32)).astype(BF16)], axis=1)


def entries_of(row_ids, sketch_bits):
    z, y, c = (lax.axis_index(a).astype(jnp.int32) for a in ("z", "y", "core"))

    def at_own(entries):
        by_owner = entries[0].reshape(BAG, -1, SB).transpose(1, 0, 2).reshape(NX, NZ, NY, NC, BAG, SB)
        part = lax.dynamic_slice(by_owner, (0, z, 0, c, 0, 0), (NX, 1, NY, 1, BAG, SB))
        return part.reshape(NX, NY, BAG, SB)

    row, bits = at_own(row_ids), at_own(sketch_bits)
    steps = ((z - (row >> 10)) * (1 - 2 * c)) & (NZ - 1)
    crossed = ((row >> 7) & 1) ^ c
    beyond = steps > NZ // 2
    ends = (steps & (NZ // 2 - 1)) == 0
    other = jnp.where(ends, crossed, beyond.astype(jnp.int32))
    near_core = jnp.where(ends, 0, crossed ^ other)
    k = jnp.where(beyond, NZ - steps, steps)
    spot = jnp.where(k == 0, 0, (2 * k - 1 + near_core) * RB) + (row & (RB - 1))
    spot = jnp.where(((row >> 8) & (NY - 1)) == y, spot, -1)
    return spot, ((2 * bits - 1) * (1 + (RADIX - 1) * other)).astype(F32)


def counts_kernel(spot_ref, value_ref, out_ref):
    rows16 = lax.broadcasted_iota(jnp.int32, (16, SB), 0).astype(jnp.int16)
    for dx in range(NX):
        spots = [jnp.broadcast_to(spot_ref[dx, k : k + 1], (16, SB)).astype(jnp.int16) for k in range(BAG)]
        values = [jnp.broadcast_to(value_ref[dx, k : k + 1], (16, SB)).astype(BF16) for k in range(BAG)]
        columns = slice(dx * SB, (dx + 1) * SB)

        def step(r, carry):
            here = rows16 + (r * 16).astype(jnp.int16)
            terms = [jnp.where(s == here, v, BF16(0)) for s, v in zip(spots, values)]
            while len(terms) > 1:
                terms = [a + b for a, b in zip(terms[::2], terms[1::2])]
            high = (terms[0] * BF16(1.0 / RADIX) + BF16(192)) - BF16(192)
            at = pl.multiple_of(r * 16, 16)
            out_ref[pl.ds(at, 16), columns] = terms[0] - high * BF16(RADIX)
            out_ref[pl.ds(HALF_ROWS + at, 16), columns] = high
            return carry

        lax.fori_loop(0, HALF_ROWS // 16, step, 0, unroll=16)


def counts_of(entries, group, *after):
    vm = pl.BlockSpec(memory_space=pltpu.VMEM)
    spec = pl.BlockSpec((None, NX, BAG, SB), lambda i: (group, 0, 0, 0))
    return pl.pallas_call(
        lambda s, v, *rest: counts_kernel(s, v, rest[-1]),
        grid=(1,),
        in_specs=[spec, spec] + [pl.BlockSpec(memory_space=pl.ANY)] * len(after),
        out_specs=pl.BlockSpec(memory_space=pltpu.VMEM),
        out_shape=jax.ShapeDtypeStruct((NC * HALF_ROWS, SAMPLES_Y), BF16),
        compiler_params=VMEM,
        cost_estimate=SMALL,
    )(*entries, *after)


def copy_kernel(a, *refs):
    refs[-1][...] = a[...]


def pair_kernel(own, other, out):
    out[:RB] = own[...]
    out[RB:] = other[...]


def onward_kernel(three, *refs):
    refs[-1][...] = three[:RB]


def rows_kernel(pair, one, two, three, four, *refs):
    out = refs[-1]
    out[:RB] = pair[:RB]
    for i, ref in enumerate((one, two, three)):
        out[(2 * i + 1) * RB : (2 * i + 3) * RB] = ref[...]
    out[7 * RB :] = four[...]


def call_after(kernel, out_shapes, operands, after):
    vm, anywhere = pl.BlockSpec(memory_space=pltpu.VMEM), pl.BlockSpec(memory_space=pl.ANY)
    return pl.pallas_call(
        kernel,
        in_specs=[vm] * len(operands) + [anywhere] * len(after),
        out_specs=[vm] * len(out_shapes),
        out_shape=[jax.ShapeDtypeStruct(s, F32) for s in out_shapes],
        compiler_params=VMEM,
        cost_estimate=SMALL,
    )(*operands, *after)


def turned_terms(rows):
    turned = rows.T
    high = turned.astype(BF16)
    return jnp.concatenate([high, (turned - high.astype(F32)).astype(BF16)], axis=0)


def pool_part(terms, count_rows):
    part = jnp.dot(terms, count_rows, preferred_element_type=F32)
    return part[:E] + part[E:]


def pool_own_kernel(rows, c0, c1, c2, c3, out):
    terms = turned_terms(rows[...])
    for x, c in enumerate((c0, c1, c2, c3)):
        out[x] = pool_part(terms, c[:HALF_ROWS])


def pool_other_kernel(rows, base, c0, c1, c2, c3, out):
    flip = own_flip()
    terms = turned_terms(rows[...])
    for x, c in enumerate((c0, c1, c2, c3)):
        total = base[x] + pool_part(terms, c[HALF_ROWS:])
        for y in range(NY):
            out[(y * NX + x) ^ flip] = total[:, y * SB : (y + 1) * SB].T


def cross_kernel(parts, u, v, bias, cot, crossed, out):
    flip = own_flip()
    x = [sum(parts[(y * NX + t) ^ flip] for y in range(1, NY)) + parts[t ^ flip] for t in range(NX)]
    base_x = jnp.concatenate(x, axis=1)
    low = jnp.dot(base_x.astype(BF16), u[...], preferred_element_type=F32).astype(BF16)
    scale = jnp.dot(low, v[...], preferred_element_type=F32) + bias[...]
    crossed[...] = (base_x * scale + base_x).astype(BF16)
    upstream = cot[...].astype(F32)
    mixed = (upstream * base_x).astype(BF16)
    last = (((1,), (1,)), ((), ()))
    back_low = lax.dot_general(mixed, v[...], last, preferred_element_type=F32).astype(BF16)
    grad_x = upstream * (scale + 1.0) + lax.dot_general(
        back_low, u[...], last, preferred_element_type=F32
    )
    for t in range(NX):
        for y in range(NY):
            out[(y * NX + t) ^ flip] = grad_x[:, t * E : (t + 1) * E]


def rows_grads(rows, terms, counts):
    total = None
    for x, c in enumerate(counts):
        part = jnp.dot(c[rows], terms[x], preferred_element_type=F32)
        total = part if total is None else total + part
    return total[:, :E] + total[:, E:]


def other_grads_kernel(g, c0, c1, c2, c3, out, terms):
    flip = own_flip()
    for x in range(NX):
        for y in range(NY):
            terms[x, y * SB : (y + 1) * SB] = split_terms(g[(y * NX + x) ^ flip])
    out[...] = rows_grads(slice(HALF_ROWS, NC * HALF_ROWS), terms, (c0, c1, c2, c3))


def own_grads_kernel(terms, c0, c1, c2, c3, out):
    out[...] = rows_grads(slice(0, HALF_ROWS), terms, (c0, c1, c2, c3))


def sums_kernel(a, b, four, two, one, three, keep):
    keep[...] = a[:RB] + b[:RB]
    for i, ref in enumerate((one, two, three)):
        s = slice((2 * i + 1) * RB, (2 * i + 3) * RB)
        ref[...] = a[s] + b[s]
    four[...] = a[7 * RB :] + b[7 * RB :]


def relay_kernel(three, four, out):
    out[:RB] = three[:RB] + four[...]
    out[RB:] = three[RB:]


def last_sums_kernel(three, two, one, keep, mine, other):
    mine[...] = keep[...] + (one[:RB] + two[:RB] + three[:RB])
    other[...] = one[RB:] + two[RB:] + three[RB:]


def update_kernel(a, b, rows, accum, new_rows, new_accum):
    grad = a[...] + b[...]
    mean = jnp.sum(grad * grad, axis=1, keepdims=True) * (1.0 / E)
    mean_row = jnp.broadcast_to(mean, (RB, E)).T[:1]
    total = accum[...] + mean_row
    new_accum[...] = total
    total_column = jnp.broadcast_to(total, (E, RB)).T
    new_rows[...] = rows[:RB] - learn_rate * grad / jnp.sqrt(total_column)


def per_device(
    table_rows, row_accum, row_ids, sketch_bits, cross_u, cross_v, cross_bias, cotangent
):
    own = table_rows[0]

    other = move(own, "core", 1)
    (held,) = call(copy_kernel, [((RB, E), F32)], own)
    (pair,) = call(pair_kernel, [((2 * RB, E), F32)], held, other)
    three, two, one = (move_ways(pair, "z", s) for s in (3, 2, 1))
    entries = entries_of(row_ids, sketch_bits)
    counts = [counts_of(entries, x) for x in range(2)]
    (onward,) = call_after(onward_kernel, [(RB, E)], (three,), counts)
    four = move_ways(onward, "z", 1)
    counts = counts + [counts_of(entries, x, onward) for x in range(2, NX)]
    (rows,) = call_after(rows_kernel, [(HALF_ROWS, E)], (pair, one, two, three, four), counts)
    other_rows = move(rows, "core", 1)
    (bags,) = call(pool_own_kernel, [((NX, E, SAMPLES_Y), F32)], rows, *counts)
    blocks = ((NX * NY, SB, E), F32)
    (bags,) = call(pool_other_kernel, [blocks], other_rows, bags, *counts)

    crossed, bag_grads = call(
        cross_kernel,
        [(cotangent.shape, BF16), blocks],
        exchange(bags),
        cross_u,
        cross_v,
        cross_bias.reshape(1, -1),
        cotangent,
    )
    bag_grads = exchange(bag_grads)
    block, pair_shape, half = (((n * RB, E), F32) for n in (1, 2, 8))
    terms_shape = ((NX, SAMPLES_Y, 2 * E), BF16)
    other_grads, terms = call(
        other_grads_kernel, [half, terms_shape], bag_grads, *counts
    )
    from_core = move(other_grads, "core", 1)
    (own_grads,) = call(own_grads_kernel, [half], terms, *counts)
    four, two, one, three, keep = call(
        sums_kernel, [block, pair_shape, pair_shape, pair_shape, block], own_grads, from_core
    )
    four_in, two_in, one_in = (move_ways(v, "z", -s) for v, s in ((four, 1), (two, 2), (one, 1)))
    (three,) = call(relay_kernel, [pair_shape], three, four_in)
    three_in = move_ways(three, "z", -3)
    mine, others = call(last_sums_kernel, [block] * 2, three_in, two_in, one_in, keep)
    new_rows, new_accum = call(
        update_kernel, [block, ((1, RB), F32)], mine, move(others, "core", 1), pair, row_accum
    )
    return (crossed, new_rows[None], new_accum)


def solution(mesh):
    grid = Mesh(mesh.devices.reshape(NX, NZ, NY, NC), ("hst", "z", "y", "core"))
    local = ("z", "y", "core")
    in_specs = (
        P("hst", local, None),
        P("hst", local),
        P("hst", None, None),
        P("hst", None, None),
        P(),
        P(),
        P(),
        P(("hst",) + local, None),
    )
    out_specs = (P(("hst",) + local, None), P("hst", local, None), P("hst", local))
    return jax.shard_map(
        per_device, mesh=grid, in_specs=in_specs, out_specs=out_specs, check_vma=False
    )
```

```python
import functools

import jax
import jax.numpy as jnp
from jax import lax
from jax.experimental import pallas as pl
from jax.experimental.pallas import tpu as pltpu
from jax.sharding import Mesh, PartitionSpec as P

learn_rate = 0.1
NX, NZ, NY, NC = 4, 8, 4, 2
RB, SB, E, BAG = 128, 128, 128, 8
SIZES = {"hst": NX, "z": NZ, "y": NY, "core": NC}
HALF_ROWS = NZ * RB
RADIX = 17
FLIP = 10
SAMPLES_Y = NX * SB
F32, BF16 = jnp.float32, jnp.bfloat16
VMEM = pltpu.CompilerParams(vmem_limit_bytes=40 << 20)
SMALL = pl.CostEstimate(flops=0, bytes_accessed=1024, transcendentals=0)


def move(array, axis, step):
    n = SIZES[axis]
    return lax.ppermute(array, axis, [(i, (i + step) % n) for i in range(n)])


def move_ways(array, axis, step):
    n = SIZES[axis]
    pairs = [
        (i * NC + c, (i + (step if c == 0 else -step)) % n * NC + c) for i in range(n) for c in range(NC)
    ]
    return lax.ppermute(array, (axis, "core"), pairs)


def call(kernel, out_shapes, *operands):
    vm = pl.BlockSpec(memory_space=pltpu.VMEM)
    return pl.pallas_call(
        kernel,
        in_specs=[vm] * len(operands),
        out_specs=[vm] * len(out_shapes),
        out_shape=[jax.ShapeDtypeStruct(s, d) for s, d in out_shapes],
        compiler_params=VMEM,
        cost_estimate=SMALL,
    )(*operands)


def own_flip():
    return lax.axis_index("core").astype(jnp.int32) * FLIP


def exchange(parts):
    groups = []
    for z in range(NZ):
        for c in range(NC):
            places = [place ^ (FLIP * c) for place in range(NX * NY)]
            groups.append([((p % NX * NZ + z) * NY + p // NX) * NC + c for p in places])
    return lax.all_to_all(
        parts, ("hst", "z", "y", "core"), split_axis=0, concat_axis=0, tiled=True, axis_index_groups=groups
    )


def split_terms(value):
    high = value.astype(BF16)
    return jnp.concatenate([high, (value - high.astype(F32)).astype(BF16)], axis=1)


def entries_of(row_ids, sketch_bits):
    z, y, c = (lax.axis_index(a).astype(jnp.int32) for a in ("z", "y", "core"))

    def at_own(entries):
        by_owner = entries[0].reshape(BAG, -1, SB).transpose(1, 0, 2).reshape(NX, NZ, NY, NC, BAG, SB)
        part = lax.dynamic_slice(by_owner, (0, z, 0, c, 0, 0), (NX, 1, NY, 1, BAG, SB))
        return part.reshape(NX, NY, BAG, SB)

    row, bits = at_own(row_ids), at_own(sketch_bits)
    steps = ((z - (row >> 10)) * (1 - 2 * c)) & (NZ - 1)
    crossed = ((row >> 7) & 1) ^ c
    beyond = steps > NZ // 2
    ends = (steps & (NZ // 2 - 1)) == 0
    other = jnp.where(ends, crossed, beyond.astype(jnp.int32))
    near_core = jnp.where(ends, 0, crossed ^ other)
    k = jnp.where(beyond, NZ - steps, steps)
    spot = jnp.where(k == 0, 0, (2 * k - 1 + near_core) * RB) + (row & (RB - 1))
    spot = jnp.where(((row >> 8) & (NY - 1)) == y, spot, -1)
    return spot, ((2 * bits - 1) * (1 + (RADIX - 1) * other)).astype(F32)


def counts_kernel(spot_ref, value_ref, out_ref):
    rows16 = lax.broadcasted_iota(jnp.int32, (16, SB), 0).astype(jnp.int16)
    for dx in range(NX):
        spots = [jnp.broadcast_to(spot_ref[dx, k : k + 1], (16, SB)).astype(jnp.int16) for k in range(BAG)]
        values = [jnp.broadcast_to(value_ref[dx, k : k + 1], (16, SB)).astype(BF16) for k in range(BAG)]
        columns = slice(dx * SB, (dx + 1) * SB)

        def step(r, carry):
            here = rows16 + (r * 16).astype(jnp.int16)
            terms = [jnp.where(s == here, v, BF16(0)) for s, v in zip(spots, values)]
            while len(terms) > 1:
                terms = [a + b for a, b in zip(terms[::2], terms[1::2])]
            high = (terms[0] * BF16(1.0 / RADIX) + BF16(192)) - BF16(192)
            at = pl.multiple_of(r * 16, 16)
            out_ref[pl.ds(at, 16), columns] = terms[0] - high * BF16(RADIX)
            out_ref[pl.ds(HALF_ROWS + at, 16), columns] = high
            return carry

        lax.fori_loop(0, HALF_ROWS // 16, step, 0, unroll=16)


def counts_of(entries, group, *after):
    vm = pl.BlockSpec(memory_space=pltpu.VMEM)
    spec = pl.BlockSpec((None, NX, BAG, SB), lambda i: (group, 0, 0, 0))
    return pl.pallas_call(
        lambda s, v, *rest: counts_kernel(s, v, rest[-1]),
        grid=(1,),
        in_specs=[spec, spec] + [pl.BlockSpec(memory_space=pl.ANY)] * len(after),
        out_specs=pl.BlockSpec(memory_space=pltpu.VMEM),
        out_shape=jax.ShapeDtypeStruct((NC * HALF_ROWS, SAMPLES_Y), BF16),
        compiler_params=VMEM,
        cost_estimate=SMALL,
    )(*entries, *after)


def copy_kernel(a, *refs):
    refs[-1][...] = a[...]


def pair_kernel(own, other, out):
    out[:RB] = own[...]
    out[RB:] = other[...]


def onward_kernel(three, *refs):
    refs[-1][...] = three[:RB]


def rows_kernel(pair, one, two, three, four, *refs):
    out = refs[-1]
    out[:RB] = pair[:RB]
    for i, ref in enumerate((one, two, three)):
        out[(2 * i + 1) * RB : (2 * i + 3) * RB] = ref[...]
    out[7 * RB :] = four[...]


def call_after(kernel, out_shapes, operands, after):
    vm, anywhere = pl.BlockSpec(memory_space=pltpu.VMEM), pl.BlockSpec(memory_space=pl.ANY)
    return pl.pallas_call(
        kernel,
        in_specs=[vm] * len(operands) + [anywhere] * len(after),
        out_specs=[vm] * len(out_shapes),
        out_shape=[jax.ShapeDtypeStruct(s, F32) for s in out_shapes],
        compiler_params=VMEM,
        cost_estimate=SMALL,
    )(*operands, *after)


def turned_terms(rows):
    turned = rows.T
    high = turned.astype(BF16)
    return jnp.concatenate([high, (turned - high.astype(F32)).astype(BF16)], axis=0)


def pool_part(terms, count_rows):
    part = jnp.dot(terms, count_rows, preferred_element_type=F32)
    return part[:E] + part[E:]


def pool_own_kernel(rows, c0, c1, c2, c3, out):
    terms = turned_terms(rows[...])
    for x, c in enumerate((c0, c1, c2, c3)):
        out[x] = pool_part(terms, c[:HALF_ROWS])


def pool_other_kernel(rows, base, c0, c1, c2, c3, out):
    flip = own_flip()
    terms = turned_terms(rows[...])
    for x, c in enumerate((c0, c1, c2, c3)):
        total = base[x] + pool_part(terms, c[HALF_ROWS:])
        for y in range(NY):
            out[(y * NX + x) ^ flip] = total[:, y * SB : (y + 1) * SB].T


def cross_kernel(parts, u, v, bias, cot, crossed, out):
    flip = own_flip()
    x = [sum(parts[(y * NX + t) ^ flip] for y in range(1, NY)) + parts[t ^ flip] for t in range(NX)]
    base_x = jnp.concatenate(x, axis=1)
    low = jnp.dot(base_x.astype(BF16), u[...], preferred_element_type=F32).astype(BF16)
    scale = jnp.dot(low, v[...], preferred_element_type=F32) + bias[...]
    crossed[...] = (base_x * scale + base_x).astype(BF16)
    upstream = cot[...].astype(F32)
    mixed = (upstream * base_x).astype(BF16)
    last = (((1,), (1,)), ((), ()))
    back_low = lax.dot_general(mixed, v[...], last, preferred_element_type=F32).astype(BF16)
    grad_x = upstream * (scale + 1.0) + lax.dot_general(
        back_low, u[...], last, preferred_element_type=F32
    )
    for t in range(NX):
        for y in range(NY):
            out[(y * NX + t) ^ flip] = grad_x[:, t * E : (t + 1) * E]


def rows_grads(rows, terms, counts):
    total = None
    for x, c in enumerate(counts):
        part = jnp.dot(c[rows], terms[x], preferred_element_type=F32)
        total = part if total is None else total + part
    return total[:, :E] + total[:, E:]


def other_grads_kernel(g, c0, c1, c2, c3, out, terms):
    flip = own_flip()
    for x in range(NX):
        for y in range(NY):
            terms[x, y * SB : (y + 1) * SB] = split_terms(g[(y * NX + x) ^ flip])
    out[...] = rows_grads(slice(HALF_ROWS, NC * HALF_ROWS), terms, (c0, c1, c2, c3))


def own_grads_kernel(terms, c0, c1, c2, c3, out):
    out[...] = rows_grads(slice(0, HALF_ROWS), terms, (c0, c1, c2, c3))


def sums_kernel(a, b, four, two, one, three, keep):
    keep[...] = a[:RB] + b[:RB]
    for i, ref in enumerate((one, two, three)):
        s = slice((2 * i + 1) * RB, (2 * i + 3) * RB)
        ref[...] = a[s] + b[s]
    four[...] = a[7 * RB :] + b[7 * RB :]


def relay_kernel(three, four, out):
    out[:RB] = three[:RB] + four[...]
    out[RB:] = three[RB:]


def last_sums_kernel(three, two, one, keep, mine, other):
    mine[...] = keep[...] + (one[:RB] + two[:RB] + three[:RB])
    other[...] = one[RB:] + two[RB:] + three[RB:]


def update_kernel(a, b, rows, accum, new_rows, new_accum):
    grad = a[...] + b[...]
    mean = jnp.sum(grad * grad, axis=1, keepdims=True) * (1.0 / E)
    mean_row = jnp.broadcast_to(mean, (RB, E)).T[:1]
    total = accum[...] + mean_row
    new_accum[...] = total
    total_column = jnp.broadcast_to(total, (E, RB)).T
    new_rows[...] = rows[:RB] - learn_rate * grad / jnp.sqrt(total_column)


def per_device(
    table_rows, row_accum, row_ids, sketch_bits, cross_u, cross_v, cross_bias, cotangent
):
    own = table_rows[0]

    other = move(own, "core", 1)
    (held,) = call(copy_kernel, [((RB, E), F32)], own)
    (pair,) = call(pair_kernel, [((2 * RB, E), F32)], held, other)
    three = move_ways(pair, "z", 3)
    entries = entries_of(row_ids, sketch_bits)
    counts = [counts_of(entries, x) for x in range(2)]
    (later,) = call_after(copy_kernel, [(2 * RB, E)], (pair,), counts)
    two, one = (move_ways(later, "z", s) for s in (2, 1))
    (onward,) = call_after(onward_kernel, [(RB, E)], (three,), counts)
    four = move_ways(onward, "z", 1)
    counts = counts + [counts_of(entries, x, onward) for x in range(2, NX)]
    (rows,) = call_after(rows_kernel, [(HALF_ROWS, E)], (pair, one, two, three, four), counts)
    other_rows = move(rows, "core", 1)
    (bags,) = call(pool_own_kernel, [((NX, E, SAMPLES_Y), F32)], rows, *counts)
    blocks = ((NX * NY, SB, E), F32)
    (bags,) = call(pool_other_kernel, [blocks], other_rows, bags, *counts)

    crossed, bag_grads = call(
        cross_kernel,
        [(cotangent.shape, BF16), blocks],
        exchange(bags),
        cross_u,
        cross_v,
        cross_bias.reshape(1, -1),
        cotangent,
    )
    bag_grads = exchange(bag_grads)
    block, pair_shape, half = (((n * RB, E), F32) for n in (1, 2, 8))
    terms_shape = ((NX, SAMPLES_Y, 2 * E), BF16)
    other_grads, terms = call(
        other_grads_kernel, [half, terms_shape], bag_grads, *counts
    )
    from_core = move(other_grads, "core", 1)
    (own_grads,) = call(own_grads_kernel, [half], terms, *counts)
    four, two, one, three, keep = call(
        sums_kernel, [block, pair_shape, pair_shape, pair_shape, block], own_grads, from_core
    )
    four_in, two_in, one_in = (move_ways(v, "z", -s) for v, s in ((four, 1), (two, 2), (one, 1)))
    (three,) = call(relay_kernel, [pair_shape], three, four_in)
    three_in = move_ways(three, "z", -3)
    mine, others = call(last_sums_kernel, [block] * 2, three_in, two_in, one_in, keep)
    new_rows, new_accum = call(
        update_kernel, [block, ((1, RB), F32)], mine, move(others, "core", 1), pair, row_accum
    )
    return (crossed, new_rows[None], new_accum)


def solution(mesh):
    grid = Mesh(mesh.devices.reshape(NX, NZ, NY, NC), ("hst", "z", "y", "core"))
    local = ("z", "y", "core")
    in_specs = (
        P("hst", local, None),
        P("hst", local),
        P("hst", None, None),
        P("hst", None, None),
        P(),
        P(),
        P(),
        P(("hst",) + local, None),
    )
    out_specs = (P(("hst",) + local, None), P("hst", local, None), P("hst", local))
    return jax.shard_map(
        per_device, mesh=grid, in_specs=in_specs, out_specs=out_specs, check_vma=False
    )
```
